128 devices in a mesh: section: 4 (over x), seq: 32 (over z, y, core).
Axes of the slice: x: 4, y: 4, z: 4, core: 2. Of those that a mesh axis runs over, the one named last changes fastest.
Arguments:
- stream: float32 [4, 4096, 1024], P('section', 'seq'), may hold values from -40 to 40
- norm_gain: float32 [4, 1024], P('section'), may hold values from 0.1 to 1.9
- w_query: bfloat16 [4, 1024, 1024], P('section'), may hold values from -0.1875 to 0.1875
- w_key: bfloat16 [4, 1024, 1024], P('section'), may hold values from -0.1875 to 0.1875
- w_value: bfloat16 [4, 1024, 2048], P('section'), may hold values from -0.1875 to 0.1875
- w_beta: bfloat16 [4, 1024, 16], P('section'), may hold values from -0.1875 to 0.1875
- w_decay: bfloat16 [4, 1024, 16], P('section'), may hold values from -0.1875 to 0.1875
- a_log: float32 [4, 16], P('section'), may hold values from -13 to -3
- dt_bias: float32 [4, 16], P('section'), may hold values from -1.5 to 1.5
- beta_bias: float32 [4, 16], P('section'), may hold values from -7 to -1
- head_gain: float32 [4, 128], P('section'), may hold values from 0.1 to 1.9
- w_output: bfloat16 [4, 2048, 1024], P('section'), may hold values from -0.125 to 0.125
- carry_state: float32 [4, 16, 128, 128], P('section'), may hold values from -6 to 6
Outputs:
- next_stream: float32 [4, 4096, 1024], P('section', 'seq')
- boundary_states: float32 [4, 32, 16, 128, 128], P('section', 'seq')
The draws below stay inside these ranges and needn't reach their ends.
All inputs are finite; a program needn't handle non-finite values.
Results may differ from the reference program's by a relative error of at most 0.0022.
Values sent between devices are 32-bit elements; how exact they have to be, the bound alone decides.
No kernel may reach another device: no remote copies, remote signals or barrier semaphores. Data moves between devices by JAX's collectives and lax.ppermute only.
A program may use at most 192 MiB of HBM per device.

```python
import jax
import jax.numpy as jnp
from jax import lax

D = 1024
KH = 8
VH = 16
DK = 128
DV = 128
BLOCK = 128
TOK_DEV = 128
SECTIONS = 4
TOKENS = 4096


def head_memory(key):
    return jax.random.uniform(key, (SECTIONS, VH), jnp.float32)


def draw_a_log(key, part):
    memory = head_memory(key)
    key = jax.random.fold_in(key, 11)
    jitter = jax.random.uniform(key, (SECTIONS, VH), jnp.float32, -1.0, 1.0)
    return -3.5 - 9.0 * memory + 0.5 * jitter


def draw_beta_bias(key, part):
    memory = head_memory(key)
    key = jax.random.fold_in(key, 12)
    jitter = jax.random.uniform(key, (SECTIONS, VH), jnp.float32, -1.0, 1.0)
    return -1.5 - 5.0 * memory + 0.5 * jitter


def draw_stream(key, part):
    key = jax.random.fold_in(key, 13)
    row_key, column_key, entry_key = jax.random.split(key, 3)
    row_scale = jnp.exp(jax.random.uniform(row_key, (SECTIONS, TOKENS, 1), jnp.float32, jnp.log(0.3), jnp.log(3.0)))
    column_scale = jnp.exp(jax.random.uniform(column_key, (SECTIONS, 1, D), jnp.float32, jnp.log(0.3), jnp.log(3.0)))
    entries = jnp.clip(jax.random.normal(entry_key, (SECTIONS, TOKENS, D), jnp.float32), -4.0, 4.0)
    return entries * row_scale * column_scale


def level_of(stream_key, shape, cuts, smallest, largest):
    def one(position, parts):
        draws = jax.random.uniform(jax.random.fold_in(jax.random.fold_in(stream_key, 6), position), (parts,), jnp.float32, smallest / len(cuts), largest / len(cuts))
        return jnp.repeat(jnp.exp(draws), shape[position] // parts).reshape((-1,) + (1,) * (len(shape) - position - 1))

    factor_of = one(*cuts[0])
    for cut in cuts[1:]:
        factor_of = factor_of * one(*cut)
    return factor_of


def noise(own_key, dims, scale, limit, cuts=(), kind=jnp.bfloat16):
    result = scale * jax.random.normal(own_key, dims, jnp.float32)
    if cuts:
        result = result * level_of(own_key, dims, cuts, -0.22, 0.18)
    return jnp.clip(result, -limit, limit).astype(kind)


def setup_inputs(seed: int = 0) -> dict:
    keys = jax.random.split(jax.random.key(seed), 14)
    stream = draw_stream(jax.random.fold_in(keys[13], 71), 0)
    norm_gain = jnp.clip(1.0 + 0.18 * jax.random.normal(keys[1], (SECTIONS, D), jnp.float32), 0.1, 1.9)
    w_query = noise(keys[2], (SECTIONS, D, KH * DK), D ** -0.5, 0.1875, ((0, 4),))
    w_key = noise(keys[3], (SECTIONS, D, KH * DK), D ** -0.5, 0.1875, ((0, 4),))
    w_value = noise(keys[4], (SECTIONS, D, VH * DV), D ** -0.5, 0.1875, ((0, 4),))
    w_beta = noise(keys[5], (SECTIONS, D, VH), D ** -0.5, 0.1875, ((0, 4),))
    w_decay = noise(keys[6], (SECTIONS, D, VH), D ** -0.5, 0.1875, ((0, 4),))
    a_log = draw_a_log(jax.random.fold_in(keys[13], 71), 0)
    dt_bias = jnp.clip(jax.random.uniform(keys[8], (SECTIONS, VH), jnp.float32, -1.5, 1.5) * level_of(keys[8], (SECTIONS, VH), ((0, 4),), -0.4, 0.0), -1.5, 1.5)
    beta_bias = draw_beta_bias(jax.random.fold_in(keys[13], 71), 0)
    head_gain = jnp.clip(1.0 + 0.18 * jax.random.normal(keys[10], (SECTIONS, DV), jnp.float32), 0.1, 1.9)
    w_output = noise(keys[11], (SECTIONS, VH * DV, D), (VH * DV) ** -0.5, 0.125, ((0, 4),))
    carry_state = noise(keys[12], (SECTIONS, VH, DK, DV), 1.0, 6.0, ((0, 4),), jnp.float32)
    return {"stream": stream, "norm_gain": norm_gain, "w_query": w_query, "w_key": w_key, "w_value": w_value, "w_beta": w_beta, "w_decay": w_decay, "a_log": a_log, "dt_bias": dt_bias, "beta_bias": beta_bias, "head_gain": head_gain, "w_output": w_output, "carry_state": carry_state}


highest = lax.Precision.HIGHEST

def normalize_rows(values, scale_row, epsilon):
    mean_square = lax.optimization_barrier(jnp.mean(values * values, axis=-1, keepdims=True))
    return values * lax.rsqrt(mean_square + epsilon) * scale_row

def unit_heads(values, head_count):
    shaped = values.reshape(values.shape[0], head_count, -1)
    return shaped * lax.rsqrt(lax.optimization_barrier(jnp.sum(shaped * shaped, axis=-1, keepdims=True)) + 1e-06)

def project(stream_rows, norm_row, query_weight, key_weight, value_weight, beta_weight, decay_weight, log_rate, decay_bias, update_bias):
    normed = normalize_rows(stream_rows, norm_row, 1e-06).astype(jnp.bfloat16)
    query_heads = unit_heads(jax.nn.silu(jnp.dot(normed.astype(jnp.float32), query_weight.astype(jnp.float32), preferred_element_type=jnp.float32)), KH) * DK ** (-0.5)
    key_heads = unit_heads(jax.nn.silu(jnp.dot(normed.astype(jnp.float32), key_weight.astype(jnp.float32), preferred_element_type=jnp.float32)), KH)
    query_heads = jnp.repeat(query_heads, VH // KH, axis=1)
    key_heads = jnp.repeat(key_heads, VH // KH, axis=1)
    value_heads = jax.nn.silu(jnp.dot(normed.astype(jnp.float32), value_weight.astype(jnp.float32), preferred_element_type=jnp.float32)).reshape(-1, VH, DV)
    strength = jax.nn.sigmoid(jnp.dot(normed.astype(jnp.float32), beta_weight.astype(jnp.float32), preferred_element_type=jnp.float32) + update_bias)
    log_decay = -jnp.exp(log_rate) * jax.nn.softplus(jnp.dot(normed.astype(jnp.float32), decay_weight.astype(jnp.float32), preferred_element_type=jnp.float32) + decay_bias)
    return (query_heads, key_heads, value_heads, strength, log_decay)

def to_blocks(values):
    blocks = values.shape[0] // BLOCK
    if values.ndim == 3:
        return values.reshape(blocks, BLOCK, values.shape[1], values.shape[2]).transpose(2, 0, 1, 3)
    return values.reshape(blocks, BLOCK, values.shape[1]).transpose(2, 0, 1)

def block_parts(query_heads, key_heads, value_heads, strength, log_decay):
    running = jnp.cumsum(log_decay, axis=-1)
    spread = running[..., :, None] - running[..., None, :]
    strict = jnp.tri(BLOCK, BLOCK, -1, dtype=bool)
    inclusive = jnp.tri(BLOCK, BLOCK, 0, dtype=bool)
    strict_ratio = jnp.where(strict, jnp.exp(jnp.where(strict, spread, 0.0)), 0.0)
    inclusive_ratio = jnp.where(inclusive, jnp.exp(jnp.where(inclusive, spread, 0.0)), 0.0)
    key_gram = jnp.einsum('hncd,hnsd->hncs', key_heads, key_heads, precision=highest)
    system = jnp.eye(BLOCK, dtype=key_gram.dtype) + strength[..., :, None] * strict_ratio * key_gram
    decay_now = jnp.exp(running)
    right_side = jnp.concatenate([strength[..., None] * value_heads, (strength * decay_now)[..., None] * key_heads], axis=-1)
    solved = lax.linalg.triangular_solve(system, right_side, left_side=True, lower=True, unit_diagonal=True)
    base_values = solved[..., :DV]
    key_mix = solved[..., DV:]
    scores = inclusive_ratio * jnp.einsum('hncd,hnsd->hncs', query_heads, key_heads, precision=highest)
    local_part = jnp.einsum('hncs,hnse->hnce', scores, base_values, precision=highest)
    row_reader = decay_now[..., None] * query_heads - jnp.einsum('hncs,hnsd->hncd', scores, key_mix, precision=highest)
    to_end = jnp.exp(running[..., -1:] - running)
    carried_keys = to_end[..., None] * key_heads
    drive_term = jnp.einsum('hncd,hnce->hnde', carried_keys, base_values, precision=highest)
    identity = jnp.eye(DK, dtype=key_gram.dtype)
    transition = jnp.exp(running[..., -1])[..., None, None] * identity - jnp.einsum('hncd,hnce->hnde', carried_keys, key_mix, precision=highest)
    return (local_part, row_reader, drive_term, transition)

def sweep(entering, local_part, row_reader, drive_term, transition):

    def advance(current, pieces):
        local_piece, reader_piece, drive_piece, move_piece = pieces
        emitted = local_piece + jnp.einsum('hcd,hde->hce', reader_piece, current, precision=highest)
        following = jnp.einsum('hde,hef->hdf', move_piece, current, precision=highest) + drive_piece
        return (following, (emitted, following))
    block_major = tuple((jnp.moveaxis(member, 1, 0) for member in (local_part, row_reader, drive_term, transition)))
    return lax.scan(advance, entering, block_major)

def one_section(inputs):
    stream_rows, norm_row, query_weight, key_weight, value_weight, beta_weight, decay_weight, log_rate, decay_bias, update_bias, gain_row, output_weight, initial = inputs
    projected = project(stream_rows, norm_row, query_weight, key_weight, value_weight, beta_weight, decay_weight, log_rate, decay_bias, update_bias)
    parts_list = block_parts(*[to_blocks(member) for member in projected])
    _, (emitted, states) = sweep(initial, *parts_list)
    per_shard = TOK_DEV // BLOCK
    boundary = states[per_shard - 1::per_shard]
    core_out = emitted.transpose(0, 2, 1, 3).reshape(-1, VH, DV)
    normalized = normalize_rows(core_out, gain_row, 1e-06).astype(jnp.bfloat16).reshape(core_out.shape[0], VH * DV)
    layer_out = stream_rows + jnp.dot(normalized.astype(jnp.float32), output_weight.astype(jnp.float32), preferred_element_type=jnp.float32)
    return (layer_out, boundary)

def reference(stream, norm_gain, w_query, w_key, w_value, w_beta, w_decay, a_log, dt_bias, beta_bias, head_gain, w_output, carry_state):
    layer_out, boundary_states = lax.map(one_section, (stream, norm_gain, w_query, w_key, w_value, w_beta, w_decay, a_log, dt_bias, beta_bias, head_gain, w_output, carry_state))
    return (jnp.roll(layer_out, 1, axis=0), boundary_states)
```

```python
import functools

import jax
import jax.numpy as jnp
from jax import lax
from jax.experimental import pallas as pl
from jax.experimental.pallas import tpu as pltpu
from jax.sharding import PartitionSpec as P

KH = 8
VH = 16
DK = 128
DV = 128
T = 128
HALF = 64
GROUP = 8
f32 = jnp.float32
bf16 = jnp.bfloat16
HIGHEST = lax.Precision.HIGHEST
VMEM_LIMIT = 56 * 2**20


def parts(values):
    high = values.astype(bf16)
    return high, (values - high.astype(f32)).astype(bf16)


def left_parts(values):
    return jnp.concatenate(parts(values), axis=1)


def right_parts(values):
    both = jnp.concatenate(parts(values), axis=1)
    return jnp.concatenate([both, both], axis=0)


def right_parts_t(values):
    high, low = parts(values)
    return jnp.concatenate(
        [jnp.concatenate([high, high], axis=1), jnp.concatenate([low, low], axis=1)], axis=0
    )


def mm_parts(left, right):
    both = jnp.dot(left, right, preferred_element_type=f32)
    columns = both.shape[1] // 2
    return both[:, :columns] + both[:, columns:]


def mm(left, right):
    return mm_parts(left_parts(left), right_parts(right))


def mm_t(left, right):
    both = lax.dot_general(
        left_parts(left), right_parts_t(right), (((1,), (1,)), ((), ())), preferred_element_type=f32
    )
    columns = both.shape[1] // 2
    return both[:, :columns] + both[:, columns:]


def sigmoid(values):
    return 1.0 / (1.0 + jnp.exp(-values))


def silu(values):
    return values * sigmoid(values)


def softplus(values):
    return jnp.maximum(values, 0.0) + jnp.log1p(jnp.exp(-jnp.abs(values)))


def unit(values):
    return values * lax.rsqrt(jnp.sum(values * values, axis=-1, keepdims=True) + 1e-06)


def square_iotas():
    rows = lax.broadcasted_iota(jnp.int32, (T, T), 0)
    columns = lax.broadcasted_iota(jnp.int32, (T, T), 1)
    return rows, columns


def upper_inverses(uppers):
    rows, columns = square_iotas()
    identity = (rows == columns).astype(f32)
    inside = (rows >> 3) == (columns >> 3)
    small = [jnp.where(inside, u, 0.0) for u in uppers]
    squares = [mm(n, n) for n in small]
    stacked = [mm(jnp.concatenate([s, n], axis=0), s) for s, n in zip(squares, small)]
    firsts = [identity - n + s - z[T:] for n, s, z in zip(small, squares, stacked)]
    result = [p + mm(p, z[:T]) for p, z in zip(firsts, stacked)]
    for shift in (3, 4, 5, 6):
        off = ((rows >> (shift + 1)) == (columns >> (shift + 1))) & (
            (rows >> shift) != (columns >> shift)
        )
        lefts = [left_parts(w) for w in result]
        rights = [right_parts(w) for w in result]
        middles = [
            mm_parts(left_parts(jnp.where(off, u, 0.0)), r) for u, r in zip(uppers, rights)
        ]
        result = [
            w - mm_parts(left, right_parts(m)) for w, left, m in zip(result, lefts, middles)
        ]
    return result


def maps_kernel(
    x_ref,
    gain_ref,
    wk_ref,
    wv_ref,
    wb_ref,
    wd_ref,
    rate_ref,
    dtb_ref,
    bb_ref,
    maps_ref,
    kt_ref,
    yt_ref,
    rt_ref,
    rb_ref,
    normed_ref,
    bt_s,
):
    step = pl.program_id(0)
    rows, columns = square_iotas()

    @pl.when(step == 0)
    def _():
        x = x_ref[...]
        mean_square = jnp.mean(x * x, axis=-1, keepdims=True)
        normed = (x * lax.rsqrt(mean_square + 1e-06) * gain_ref[...]).astype(bf16)
        normed_ref[...] = normed
        beta = sigmoid(jnp.dot(normed, wb_ref[...], preferred_element_type=f32) + bb_ref[...])
        log_decay = -jnp.exp(rate_ref[...]) * softplus(
            jnp.dot(normed, wd_ref[...], preferred_element_type=f32) + dtb_ref[...]
        )
        contract0 = (((0,), (0,)), ((), ()))
        lower = (rows >= columns).astype(f32)
        upper = (rows <= columns).astype(f32)
        identity = (rows == columns).astype(f32)
        running = jnp.dot(lower, log_decay, precision=HIGHEST, preferred_element_type=f32)
        rt_ref[...] = lax.dot_general(
            log_decay, upper, contract0, precision=HIGHEST, preferred_element_type=f32
        )
        bt_s[...] = lax.dot_general(
            beta, identity, contract0, precision=HIGHEST, preferred_element_type=f32
        )
        for h in range(VH):
            rb_ref[h] = jnp.broadcast_to(running[:, h : h + 1], (T, T))

    normed = normed_ref[...]
    key_all = silu(jnp.dot(normed, wk_ref[...], preferred_element_type=f32))
    value_all = silu(jnp.dot(normed, wv_ref[...], preferred_element_type=f32))
    keys = [unit(key_all[:, i * DK : (i + 1) * DK]) for i in range(GROUP // 2)]
    keys_t = [k.T for k in keys]
    for i, kt in enumerate(keys_t):
        kt_ref[i] = kt
    grams = [mm(k, kt) for k, kt in zip(keys, keys_t)]
    key_rights = [right_parts(k) for k in keys]
    strict = rows < columns
    r_rows = [rt_ref[pl.ds(step * GROUP + i, 1), :] for i in range(GROUP)]
    b_rows = [bt_s[pl.ds(step * GROUP + i, 1), :] for i in range(GROUP)]
    uppers = []
    for i in range(GROUP):
        spread = jnp.minimum(r_rows[i] - rb_ref[step * GROUP + i], 0.0)
        uppers.append(jnp.where(strict, b_rows[i] * jnp.exp(spread) * grams[i // 2], 0.0))
    inverses = upper_inverses(uppers)
    solved = []
    for i in range(GROUP):
        value_t = value_all[:, i * DV : (i + 1) * DV].T
        right_t = jnp.concatenate(
            [b_rows[i] * value_t, (b_rows[i] * jnp.exp(r_rows[i])) * keys_t[i // 2]], axis=0
        )
        solved.append(mm(right_t, inverses[i]))
        yt_ref[i] = solved[i]
    identity = rows == columns
    for i in range(GROUP):
        end = r_rows[i][:, T - 1 : T]
        both = mm_parts(left_parts(solved[i] * jnp.exp(end - r_rows[i])), key_rights[i // 2])
        maps_ref[i, 0:DK] = jnp.where(identity, jnp.exp(end), 0.0) - both[DV:]
        maps_ref[i, DK : DK + DV] = both[:DV]


def make_maps(x, gain, wk, wv, wb, wd, rate, dtb, bb):
    steps = VH // GROUP
    whole = lambda a: pl.BlockSpec(a.shape, lambda s: (0,) * a.ndim)
    return pl.pallas_call(
        maps_kernel,
        grid=(steps,),
        in_specs=[
            whole(x),
            whole(gain),
            pl.BlockSpec((wk.shape[0], KH * DK // steps), lambda s: (0, s)),
            pl.BlockSpec((wv.shape[0], VH * DV // steps), lambda s: (0, s)),
            whole(wb),
            whole(wd),
            whole(rate),
            whole(dtb),
            whole(bb),
        ],
        out_specs=[
            pl.BlockSpec((GROUP, DK + DV, DK), lambda s: (s, 0, 0)),
            pl.BlockSpec((GROUP // 2, DK, T), lambda s: (s, 0, 0)),
            pl.BlockSpec((GROUP, DK + DV, T), lambda s: (s, 0, 0)),
            pl.BlockSpec((VH, T), lambda s: (0, 0)),
            pl.BlockSpec((VH, T, T), lambda s: (0, 0, 0)),
            pl.BlockSpec((T, x.shape[1]), lambda s: (0, 0)),
        ],
        out_shape=[
            jax.ShapeDtypeStruct((VH, DK + DV, DK), f32),
            jax.ShapeDtypeStruct((KH, DK, T), f32),
            jax.ShapeDtypeStruct((VH, DK + DV, T), f32),
            jax.ShapeDtypeStruct((VH, T), f32),
            jax.ShapeDtypeStruct((VH, T, T), f32),
            jax.ShapeDtypeStruct((T, x.shape[1]), bf16),
        ],
        scratch_shapes=[pltpu.VMEM((VH, T), f32)],
        compiler_params=pltpu.CompilerParams(vmem_limit_bytes=VMEM_LIMIT),
        cost_estimate=pl.CostEstimate(
            flops=4 * 10**9, bytes_accessed=14 * 2**20, transcendentals=10**6
        ),
        name="block_maps",
    )(x, gain, wk, wv, wb, wd, rate, dtb, bb)


def readers_kernel(normed_ref, wq_ref, kt_ref, yt_ref, rt_ref, rb_ref, local_ref, reader_ref):
    step = pl.program_id(0)
    rows, columns = square_iotas()
    inclusive = rows >= columns
    query_all = silu(jnp.dot(normed_ref[...], wq_ref[...], preferred_element_type=f32))
    queries = [
        unit(query_all[:, i * DK : (i + 1) * DK]) * DK ** (-0.5) for i in range(GROUP // 2)
    ]
    products = [mm(q, kt_ref[i]) for i, q in enumerate(queries)]
    scores = []
    for i in range(GROUP):
        spread = jnp.minimum(rb_ref[i] - rt_ref[pl.ds(step * GROUP + i, 1), :], 0.0)
        scores.append(jnp.where(inclusive, jnp.exp(spread) * products[i // 2], 0.0))
    for i in range(GROUP):
        both = mm_t(scores[i], yt_ref[i])
        local_ref[i] = both[:, :DV]
        reader_ref[i] = jnp.exp(rb_ref[i]) * queries[i // 2] - both[:, DV:]


def make_readers(normed, wq, kt, yt, rt, rb):
    steps = VH // GROUP
    square = pl.BlockSpec((GROUP, T, T), lambda s: (s, 0, 0))
    return pl.pallas_call(
        readers_kernel,
        grid=(steps,),
        in_specs=[
            pl.BlockSpec(normed.shape, lambda s: (0, 0)),
            pl.BlockSpec((wq.shape[0], KH * DK // steps), lambda s: (0, s)),
            pl.BlockSpec((GROUP // 2, DK, T), lambda s: (s, 0, 0)),
            pl.BlockSpec((GROUP, DK + DV, T), lambda s: (s, 0, 0)),
            pl.BlockSpec(rt.shape, lambda s: (0, 0)),
            square,
        ],
        out_specs=[square, square],
        out_shape=[jax.ShapeDtypeStruct((VH, T, T), f32)] * 2,
        compiler_params=pltpu.CompilerParams(vmem_limit_bytes=VMEM_LIMIT),
        cost_estimate=pl.CostEstimate(
            flops=2 * 10**9, bytes_accessed=8 * 2**20, transcendentals=10**6
        ),
        name="readers",
    )(normed, wq, kt, yt, rt, rb)


def on_each_core(core_ref, body):
    for core in (0, 1):

        @pl.when(core_ref[0] == core)
        def _(core=core):
            body(core)


def compose_kernel(core_ref, own_ref, other_ref, out_ref):

    def body(core):
        first, second = (own_ref, other_ref) if core == 0 else (other_ref, own_ref)
        a_rows = slice(core * HALF, core * HALF + HALF)
        b_rows = slice(DK + core * HALF, DK + core * HALF + HALF)
        for h in range(VH):
            left = jnp.concatenate([first[h, a_rows], first[h, b_rows]], axis=0)
            both = mm(left, second[h, 0:DK])
            out_ref[h, 0:HALF] = both[:HALF]
            out_ref[h, HALF : 2 * HALF] = both[HALF:] + second[h, b_rows]

    on_each_core(core_ref, body)


def scan_kernel(core_ref, map_ref, other_ref, initial_ref, out_ref):

    def body(core):
        current = initial_ref[core * HALF : core * HALF + HALF]
        count = map_ref.shape[0]
        rights = []
        for p in range(count - 1):
            halves = [map_ref[p, 0:HALF], other_ref[p]]
            rights.append(right_parts(jnp.concatenate(halves if core == 0 else halves[::-1], axis=0)))
        for p in range(count):
            out_ref[p] = current
            if p < count - 1:
                current = mm_parts(left_parts(current), rights[p]) + map_ref[p, HALF : 2 * HALF]

    on_each_core(core_ref, body)


def enter_kernel(core_ref, state_ref, own_ref, other_ref, keep_ref, send_ref):

    def body(core):
        first = own_ref if core == 0 else other_ref
        given, moved = (keep_ref, send_ref) if core == 0 else (send_ref, keep_ref)
        b_rows = slice(DK + core * HALF, DK + core * HALF + HALF)
        for h in range(VH):
            state = state_ref[h]
            given[h] = state
            moved[h] = mm(state, first[h, 0:DK]) + first[h, b_rows]

    on_each_core(core_ref, body)


def entering_of(core_ref, keep_ref, got_ref, h):
    keep, got = keep_ref[h], got_ref[h]
    first = core_ref[0] == 0
    return jnp.concatenate([jnp.where(first, keep, got), jnp.where(first, got, keep)], axis=0)


def output_kernel(
    core_ref, keep_ref, got_ref, local_ref, reader_ref, gain_ref, x_ref, wo_ref, out_ref, wo_s, sem
):
    copy = pltpu.make_async_copy(wo_ref, wo_s, sem)
    copy.start()
    heads = []
    for h in range(VH):
        entering = entering_of(core_ref, keep_ref, got_ref, h)
        core = local_ref[h] + mm_t(reader_ref[h], entering)
        mean_square = jnp.mean(core * core, axis=-1, keepdims=True)
        heads.append((core * lax.rsqrt(mean_square + 1e-06) * gain_ref[...]).astype(bf16))
    copy.wait()
    out_ref[...] = x_ref[...] + jnp.dot(
        jnp.concatenate(heads, axis=1), wo_s[...], preferred_element_type=f32
    )


def boundary_kernel(core_ref, keep_ref, got_ref, own_ref, out_ref):
    for h in range(VH):
        entering = entering_of(core_ref, keep_ref, got_ref, h)
        out_ref[h] = (mm(entering, own_ref[h, 0:DK]) + own_ref[h, DK : DK + DV]).T


def plain_call(kernel, name, outputs, flops, bytes_accessed, arguments, in_hbm=(), scratch=()):
    vmem = pl.BlockSpec(memory_space=pltpu.VMEM)
    specs = [pl.BlockSpec(memory_space=pltpu.SMEM)] + [
        pl.BlockSpec(memory_space=pl.ANY) if i in in_hbm else vmem
        for i in range(1, len(arguments))
    ]
    several = isinstance(outputs, list)
    return pl.pallas_call(
        kernel,
        in_specs=specs,
        out_specs=[vmem] * len(outputs) if several else vmem,
        out_shape=outputs,
        scratch_shapes=scratch,
        compiler_params=pltpu.CompilerParams(vmem_limit_bytes=VMEM_LIMIT),
        cost_estimate=pl.CostEstimate(
            flops=flops, bytes_accessed=bytes_accessed, transcendentals=0
        ),
        name=name,
    )(*arguments)


def on_device(
    stream,
    norm_gain,
    w_query,
    w_key,
    w_value,
    w_beta,
    w_decay,
    a_log,
    dt_bias,
    beta_bias,
    head_gain,
    w_output,
    carry_state,
):
    count = lax.axis_size("seq")
    position = lax.axis_index("seq")
    core = (position % 2).astype(jnp.int32)[None]
    chips = count // 2
    pairs = [(i, i ^ 1) for i in range(count)]
    groups = [[2 * i + c for i in range(chips)] for c in range(2)]
    x = stream[0]
    shape = lambda *dims: jax.ShapeDtypeStruct(dims, f32)

    maps, kt, yt, rt, rb, normed = make_maps(
        x, norm_gain, w_key[0], w_value[0], w_beta[0], w_decay[0], a_log, dt_bias, beta_bias
    )
    maps_other = lax.ppermute(maps, "seq", pairs)
    local, reader = make_readers(normed, w_query[0], kt, yt, rt, rb)

    chip_maps = plain_call(
        compose_kernel, "compose", shape(VH, 2 * HALF, DK), 10**9, 5 * 2**20, (core, maps, maps_other)
    )
    gathered = lax.all_to_all(chip_maps, "seq", 0, 0, axis_index_groups=groups)
    gathered_other = lax.ppermute(gathered[:, :HALF], "seq", pairs)
    initial = lax.dynamic_index_in_dim(carry_state[0], position // 2, 0, keepdims=False).T
    states = plain_call(
        scan_kernel,
        "scan_chips",
        shape(chips, HALF, DK),
        10**8,
        2 * 2**20,
        (core, gathered, gathered_other, initial),
    )
    returned = lax.all_to_all(states, "seq", 0, 0, axis_index_groups=groups)
    keep, send = plain_call(
        enter_kernel,
        "enter",
        [shape(VH, HALF, DK)] * 2,
        10**9,
        5 * 2**20,
        (core, returned, maps, maps_other),
    )
    got = lax.ppermute(send, "seq", pairs)
    rows_out = plain_call(
        output_kernel,
        "output_rows",
        shape(*x.shape),
        3 * 10**9,
        8 * 2**20,
        (core, keep, got, local, reader, head_gain, x, w_output[0]),
        in_hbm=(7,),
        scratch=[pltpu.VMEM(w_output.shape[1:], bf16), pltpu.SemaphoreType.DMA],
    )
    sections = lax.axis_size("section")
    next_rows = lax.ppermute(rows_out, "section", [(i, (i + 1) % sections) for i in range(sections)])
    boundary = plain_call(
        boundary_kernel, "boundary", shape(VH, DK, DV), 10**9, 4 * 2**20, (core, keep, got, maps)
    )
    return (next_rows[None], boundary[None, None])


def solution(mesh):
    placed = (
        P("section", "seq", None),
        P("section", None),
        P("section", None, None),
        P("section", None, None),
        P("section", None, None),
        P("section", None, None),
        P("section", None, None),
        P("section", None),
        P("section", None),
        P("section", None),
        P("section", None),
        P("section", None, None),
        P("section", None, None, None),
    )
    return jax.shard_map(
        on_device,
        mesh=mesh,
        in_specs=placed,
        out_specs=(P("section", "seq", None), P("section", "seq", None, None, None)),
        check_vma=False,
    )
```

```python
import functools

import jax
import jax.numpy as jnp
from jax import lax
from jax.experimental import pallas as pl
from jax.experimental.pallas import tpu as pltpu
from jax.sharding import PartitionSpec as P

KH = 8
VH = 16
DK = 128
DV = 128
T = 128
HALF = 64
CHUNKS = 4
f32 = jnp.float32
bf16 = jnp.bfloat16
HIGHEST = lax.Precision.HIGHEST
MIB = 2**20
BATCH = 4


def parts(values):
    high = values.astype(bf16)
    return high, (values - high.astype(f32)).astype(bf16)


def left_parts(values):
    return jnp.concatenate(parts(values), axis=1)


def right_parts(values):
    both = jnp.concatenate(parts(values), axis=1)
    return jnp.concatenate([both, both], axis=0)


def right_parts_t(values):
    high, low = parts(values)
    return jnp.concatenate(
        [jnp.concatenate([high, high], axis=1), jnp.concatenate([low, low], axis=1)], axis=0
    )


def mm_parts(left, right):
    both = jnp.dot(left, right, preferred_element_type=f32)
    columns = both.shape[1] // 2
    return both[:, :columns] + both[:, columns:]


def mm(left, right):
    return mm_parts(left_parts(left), right_parts(right))


def mm_t(left, right):
    both = lax.dot_general(
        left_parts(left), right_parts_t(right), (((1,), (1,)), ((), ())), preferred_element_type=f32
    )
    columns = both.shape[1] // 2
    return both[:, :columns] + both[:, columns:]


def dot_t(left, right):
    return lax.dot_general(left, right, (((1,), (1,)), ((), ())), preferred_element_type=f32)


def sigmoid(values):
    return 1.0 / (1.0 + jnp.exp(-values))


def silu(values):
    return values * sigmoid(values)


def softplus(values):
    return jnp.maximum(values, 0.0) + jnp.log1p(jnp.exp(-jnp.abs(values)))


def unit(values):
    return values * lax.rsqrt(jnp.sum(values * values, axis=-1, keepdims=True) + 1e-06)


def square_iotas():
    rows = lax.broadcasted_iota(jnp.int32, (T, T), 0)
    columns = lax.broadcasted_iota(jnp.int32, (T, T), 1)
    return rows, columns


def upper_inverses(uppers):
    rows, columns = square_iotas()
    identity = (rows == columns).astype(f32)
    inside = (rows >> 3) == (columns >> 3)
    small = [jnp.where(inside, u, 0.0) for u in uppers]
    squares = [mm(n, n) for n in small]
    stacked = [mm(jnp.concatenate([s, n], axis=0), s) for s, n in zip(squares, small)]
    firsts = [identity - n + s - z[T:] for n, s, z in zip(small, squares, stacked)]
    result = [p + mm(p, z[:T]) for p, z in zip(firsts, stacked)]
    for shift in (3, 4, 5, 6):
        off = ((rows >> (shift + 1)) == (columns >> (shift + 1))) & (
            (rows >> shift) != (columns >> shift)
        )
        lefts = [left_parts(w) for w in result]
        rights = [right_parts(w) for w in result]
        middles = [
            mm_parts(left_parts(jnp.where(off, u, 0.0)), r) for u, r in zip(uppers, rights)
        ]
        result = [
            w - mm_parts(left, right_parts(m)) for w, left, m in zip(result, lefts, middles)
        ]
    return result


def column_of(row_ref):
    rows = lax.broadcasted_iota(jnp.int32, (VH, VH), 0)
    columns = lax.broadcasted_iota(jnp.int32, (VH, VH), 1)
    return jnp.sum(jnp.where(rows == columns, row_ref[...], 0.0), axis=1, keepdims=True)


def maps_kernel(
    core_ref,
    x_ref,
    gain_ref,
    wk_ref,
    wv_ref,
    wb_ref,
    wd_ref,
    rate_ref,
    dtb_ref,
    bb_ref,
    send_ref,
    own_ref,
    kt_ref,
    yt_ref,
    rt_ref,
    rb_ref,
    normed_ref,
):
    rows, columns = square_iotas()
    x = x_ref[...]
    mean_square = jnp.mean(x * x, axis=-1, keepdims=True)
    normed = (x * lax.rsqrt(mean_square + 1e-06) * gain_ref[...]).astype(bf16)
    normed_ref[...] = normed
    beta = sigmoid(dot_t(wb_ref[...], normed) + column_of(bb_ref))
    log_decay = -jnp.exp(column_of(rate_ref)) * softplus(
        dot_t(wd_ref[...], normed) + column_of(dtb_ref)
    )
    upper = (rows <= columns).astype(f32)
    running = jnp.dot(log_decay, upper, precision=HIGHEST, preferred_element_type=f32)
    rt_ref[...] = running
    r_rows = [running[h : h + 1] for h in range(VH)]
    b_rows = [beta[h : h + 1] for h in range(VH)]
    key_all = silu(jnp.dot(normed, wk_ref[...], preferred_element_type=f32))
    keys = [unit(key_all[:, i * DK : (i + 1) * DK]) for i in range(KH)]
    keys_t = [k.T for k in keys]
    for i, kt in enumerate(keys_t):
        kt_ref[i] = kt
    grams = [mm(k, kt) for k, kt in zip(keys, keys_t)]
    strict = rows < columns
    uppers = []
    for h in range(VH):
        r_columns = jnp.broadcast_to(r_rows[h], (T, T)).T
        rb_ref[h] = r_columns
        spread = jnp.minimum(r_rows[h] - r_columns, 0.0)
        uppers.append(jnp.where(strict, b_rows[h] * jnp.exp(spread) * grams[h // 2], 0.0))
    inverses = upper_inverses(uppers)
    value_all = silu(jnp.dot(normed, wv_ref[...], preferred_element_type=f32))
    solved = []
    for h in range(VH):
        value_t = value_all[:, h * DV : (h + 1) * DV].T
        right_t = jnp.concatenate(
            [b_rows[h] * value_t, (b_rows[h] * jnp.exp(r_rows[h])) * keys_t[h // 2]], axis=0
        )
        solved.append(mm(right_t, inverses[h]))
        yt_ref[h] = solved[h]
    key_rights = [right_parts(k) for k in keys]
    identity = rows == columns
    other_rows = pl.ds(pl.multiple_of((1 - core_ref[0]) * HALF, HALF), HALF)
    for h in range(VH):
        end = r_rows[h][:, T - 1 : T]
        both = mm_parts(left_parts(solved[h] * jnp.exp(end - r_rows[h])), key_rights[h // 2])
        own_ref[h] = both[:DV]
        send_ref[h, 0:DK] = jnp.where(identity, jnp.exp(end), 0.0) - both[DV:]
        send_ref[h, DK : DK + HALF] = own_ref[h, other_rows, :]


def make_maps(core, *arguments):
    x = arguments[0]
    vmem = pl.BlockSpec(memory_space=pltpu.VMEM)
    return pl.pallas_call(
        maps_kernel,
        in_specs=[pl.BlockSpec(memory_space=pltpu.SMEM)]
        + [vmem] * len(arguments),
        out_specs=[vmem] * 7,
        out_shape=[
            jax.ShapeDtypeStruct((VH, DK + HALF, DK), f32),
            jax.ShapeDtypeStruct((VH, DV, DK), f32),
            jax.ShapeDtypeStruct((KH, DK, T), f32),
            jax.ShapeDtypeStruct((VH, DK + DV, T), f32),
            jax.ShapeDtypeStruct((VH, T), f32),
            jax.ShapeDtypeStruct((VH, T, T), f32),
            jax.ShapeDtypeStruct((T, x.shape[1]), bf16),
        ],
        compiler_params=pltpu.CompilerParams(vmem_limit_bytes=20 * MIB),
        cost_estimate=pl.CostEstimate(
            flops=4 * 10**9, bytes_accessed=14 * 2**20, transcendentals=10**6
        ),
        name="block_maps",
    )(core, *arguments)


def readers_kernel(
    normed_ref, wq_hbm, kt_ref, yt_ref, rt_ref, rb_ref, local_ref, reader_ref, wq_s, sem
):
    copy = pltpu.make_async_copy(wq_hbm, wq_s, sem)
    copy.start()
    rows, columns = square_iotas()
    inclusive = rows >= columns
    copy.wait()
    query_all = silu(jnp.dot(normed_ref[...], wq_s[...], preferred_element_type=f32))
    for i in range(KH):
        query = unit(query_all[:, i * DK : (i + 1) * DK]) * DK ** (-0.5)
        product = mm(query, kt_ref[i])
        for h in (2 * i, 2 * i + 1):
            spread = jnp.minimum(rb_ref[h] - rt_ref[h : h + 1], 0.0)
            both = mm_t(jnp.where(inclusive, jnp.exp(spread) * product, 0.0), yt_ref[h])
            local_ref[h] = both[:, :DV]
            reader_ref[h] = jnp.exp(rb_ref[h]) * query - both[:, DV:]


def make_readers(normed, wq, *arguments):
    vmem = pl.BlockSpec(memory_space=pltpu.VMEM)
    return pl.pallas_call(
        readers_kernel,
        in_specs=[vmem, pl.BlockSpec(memory_space=pltpu.HBM)] + [vmem] * len(arguments),
        out_specs=[vmem, vmem],
        out_shape=[jax.ShapeDtypeStruct((VH, T, T), f32)] * 2,
        scratch_shapes=[pltpu.VMEM(wq.shape, wq.dtype), pltpu.SemaphoreType.DMA],
        compiler_params=pltpu.CompilerParams(vmem_limit_bytes=8 * MIB),
        cost_estimate=pl.CostEstimate(
            flops=2 * 10**9, bytes_accessed=8 * 2**20, transcendentals=10**6
        ),
        name="readers",
    )(normed, wq, *arguments)


def on_each_core(core_ref, body):
    for core in (0, 1):

        @pl.when(core_ref[0] == core)
        def _(core=core):
            body(core)


def initial_kernel(place_ref, carry_ref, out_ref):
    state = carry_ref[place_ref[0]].T

    @pl.when(place_ref[1] == 0)
    def _():
        out_ref[...] = state[:HALF]

    @pl.when(place_ref[1] == 1)
    def _():
        out_ref[...] = state[HALF:]


def compose_kernel(core_ref, sent_ref, own_ref, got_ref, out_ref):

    def body(core):
        mine = slice(core * HALF, core * HALF + HALF)
        for h in range(VH):
            own_b, got_b = own_ref[h, mine], got_ref[h, DK : DK + HALF]
            if core == 0:
                first_a, first_b, second_a, second_b = sent_ref, own_b, got_ref, got_b
            else:
                first_a, first_b, second_a, second_b = got_ref, got_b, sent_ref, own_b
            both = mm(jnp.concatenate([first_a[h, mine], first_b], axis=0), second_a[h, 0:DK])
            out_ref[h, 0:HALF] = both[:HALF]
            out_ref[h, HALF : 2 * HALF] = both[HALF:] + second_b

    on_each_core(core_ref, body)


def scan_kernel(core_ref, map_hbm, other_hbm, initial_ref, out_ref, map_ref, other_ref, sems):
    count = map_ref.shape[0]
    batches = [slice(p, p + BATCH) for p in range(0, count, BATCH)]
    copies = []
    for i, batch in enumerate(batches):
        copies.append(
            (
                pltpu.make_async_copy(map_hbm.at[batch], map_ref.at[batch], sems.at[2 * i]),
                pltpu.make_async_copy(
                    other_hbm.at[batch, 0:HALF], other_ref.at[batch], sems.at[2 * i + 1]
                ),
            )
        )
        for copy in copies[-1]:
            copy.start()

    def body(core):
        current = initial_ref[...]
        for p in range(count):
            if p % BATCH == 0:
                for copy in copies[p // BATCH]:
                    copy.wait()
            out_ref[p] = current
            if p < count - 1:
                halves = [map_ref[p, 0:HALF], other_ref[p]]
                right = jnp.concatenate(halves if core == 0 else halves[::-1], axis=0)
                current = mm(current, right) + map_ref[p, HALF : 2 * HALF]

    on_each_core(core_ref, body)


def enter_kernel(core_ref, state_ref, sent_ref, own_ref, got_ref, keep_ref, send_ref):

    def body(core):
        given, moved = (keep_ref, send_ref) if core == 0 else (send_ref, keep_ref)
        for h in range(VH):
            state = state_ref[h]
            given[h] = state
            if core == 0:
                moved[h] = mm(state, sent_ref[h, 0:DK]) + own_ref[h, 0:HALF]
            else:
                moved[h] = mm(state, got_ref[h, 0:DK]) + got_ref[h, DK : DK + HALF]

    on_each_core(core_ref, body)


def entering_of(core_ref, keep_ref, got_ref, h):
    keep, got = keep_ref[h], got_ref[h]
    first = core_ref[0] == 0
    return jnp.concatenate([jnp.where(first, keep, got), jnp.where(first, got, keep)], axis=0)


def output_kernel(
    core_ref, keep_ref, got_ref, local_ref, reader_ref, gain_ref, x_ref, wo_ref, out_ref, wo_s, sem
):
    copy = pltpu.make_async_copy(wo_ref, wo_s, sem)
    copy.start()
    heads = []
    for h in range(VH):
        entering = entering_of(core_ref, keep_ref, got_ref, h)
        core = local_ref[h] + mm_t(reader_ref[h], entering)
        mean_square = jnp.mean(core * core, axis=-1, keepdims=True)
        heads.append((core * lax.rsqrt(mean_square + 1e-06) * gain_ref[...]).astype(bf16))
    copy.wait()
    out_ref[...] = x_ref[...] + jnp.dot(
        jnp.concatenate(heads, axis=1), wo_s[...], preferred_element_type=f32
    )


def boundary_kernel(core_ref, keep_ref, got_ref, sent_ref, own_ref, out_ref):
    for h in range(VH):
        entering = entering_of(core_ref, keep_ref, got_ref, h)
        out_ref[h] = (mm(entering, sent_ref[h, 0:DK]) + own_ref[h]).T


def plain_call(kernel, name, outputs, flops, bytes_accessed, arguments, in_hbm=(), scratch=()):
    vmem = pl.BlockSpec(memory_space=pltpu.VMEM)
    specs = [pl.BlockSpec(memory_space=pltpu.SMEM)] + [
        pl.BlockSpec(memory_space=pl.ANY) if i in in_hbm else vmem
        for i in range(1, len(arguments))
    ]
    several = isinstance(outputs, list)
    return pl.pallas_call(
        kernel,
        in_specs=specs,
        out_specs=[vmem] * len(outputs) if several else vmem,
        out_shape=outputs,
        scratch_shapes=scratch,
        compiler_params=pltpu.CompilerParams(vmem_limit_bytes=6 * MIB),
        cost_estimate=pl.CostEstimate(
            flops=flops, bytes_accessed=bytes_accessed, transcendentals=0
        ),
        name=name,
    )(*arguments)


def on_device(
    stream,
    norm_gain,
    w_query,
    w_key,
    w_value,
    w_beta,
    w_decay,
    a_log,
    dt_bias,
    beta_bias,
    head_gain,
    w_output,
    carry_state,
):
    count = lax.axis_size("seq")
    position = lax.axis_index("seq")
    core = (position % 2).astype(jnp.int32)[None]
    chips = count // 2
    pairs = [(i, i ^ 1) for i in range(count)]
    groups = [[2 * i + c for i in range(chips)] for c in range(2)]
    x = stream[0]
    shape = lambda *dims: jax.ShapeDtypeStruct(dims, f32)

    place = jnp.stack([position // 2, position % 2]).astype(jnp.int32)
    initial = plain_call(
        initial_kernel, "initial_state", shape(HALF, DK), 10**11, 200 * 2**20, (place, carry_state[0])
    )
    core, initial = lax.optimization_barrier((core, initial))
    maps, drives, kt, yt, rt, rb, normed = make_maps(
        core,
        x,
        norm_gain,
        w_key[0],
        w_value[0],
        w_beta[0].T,
        w_decay[0].T,
        a_log,
        dt_bias,
        beta_bias,
    )
    maps_other = lax.ppermute(maps, "seq", pairs)
    local, reader = make_readers(normed, w_query[0], kt, yt, rt, rb)
    maps_other, local, reader = lax.optimization_barrier((maps_other, local, reader))

    chip_maps = plain_call(
        compose_kernel,
        "compose",
        shape(VH, 2 * HALF, DK),
        10**9,
        5 * 2**20,
        (core, maps, drives, maps_other),
    )
    gathered = lax.all_to_all(chip_maps, "seq", 0, 0, axis_index_groups=groups)
    gathered_other = lax.ppermute(gathered, "seq", pairs)
    states = plain_call(
        scan_kernel,
        "scan_chips",
        shape(chips, HALF, DK),
        10**8,
        30 * 2**20,
        (core, gathered, gathered_other, initial),
        in_hbm=(1, 2),
        scratch=[
            pltpu.VMEM((chips, 2 * HALF, DK), f32),
            pltpu.VMEM((chips, HALF, DK), f32),
            pltpu.SemaphoreType.DMA((2 * chips // BATCH,)),
        ],
    )
    returned = lax.all_to_all(states, "seq", 0, 0, axis_index_groups=groups)
    keep, send = plain_call(
        enter_kernel,
        "enter",
        [shape(VH, HALF, DK)] * 2,
        10**9,
        30 * 2**20,
        (core, returned, maps, drives, maps_other),
    )
    got = lax.ppermute(send, "seq", pairs)
    rows_out = plain_call(
        output_kernel,
        "output_rows",
        shape(*x.shape),
        3 * 10**9,
        8 * 2**20,
        (core, keep, got, local, reader, head_gain, x, w_output[0]),
        in_hbm=(7,),
        scratch=[pltpu.VMEM(w_output.shape[1:], bf16), pltpu.SemaphoreType.DMA],
    )
    sections = lax.axis_size("section")
    onward = [(i, (i + 1) % sections) for i in range(sections)]
    chunk = T // CHUNKS
    next_rows = jnp.concatenate(
        [lax.ppermute(rows_out[i * chunk : (i + 1) * chunk], "section", onward) for i in range(CHUNKS)]
    )
    boundary = plain_call(
        boundary_kernel, "boundary", shape(VH, DK, DV), 10**9, 4 * 2**20, (core, keep, got, maps, drives)
    )
    return (next_rows[None], boundary[None, None])


def solution(mesh):
    placed = (
        P("section", "seq", None),
        P("section", None),
        P("section", None, None),
        P("section", None, None),
        P("section", None, None),
        P("section", None, None),
        P("section", None, None),
        P("section", None),
        P("section", None),
        P("section", None),
        P("section", None),
        P("section", None, None),
        P("section", None, None, None),
    )
    return jax.shard_map(
        on_device,
        mesh=mesh,
        in_specs=placed,
        out_specs=(P("section", "seq", None), P("section", "seq", None, None, None)),
        check_vma=False,
    )
```

```python
import functools

import jax
import jax.numpy as jnp
from jax import lax
from jax.experimental import pallas as pl
from jax.experimental.pallas import tpu as pltpu
from jax.sharding import PartitionSpec as P

KH = 8
VH = 16
DK = 128
DV = 128
T = 128
HALF = 64
CHUNKS = 4
f32 = jnp.float32
bf16 = jnp.bfloat16
HIGHEST = lax.Precision.HIGHEST
MIB = 2**20
BATCH = 4


def parts(values):
    high = values.astype(bf16)
    return high, (values - high.astype(f32)).astype(bf16)


def left_parts(values):
    return jnp.concatenate(parts(values), axis=1)


def right_parts(values):
    both = jnp.concatenate(parts(values), axis=1)
    return jnp.concatenate([both, both], axis=0)


def mm_parts(left, right):
    both = jnp.dot(left, right, preferred_element_type=f32)
    columns = both.shape[1] // 2
    return both[:, :columns] + both[:, columns:]


def mm(left, right):
    return mm_parts(left_parts(left), right_parts(right))


def mm_t(left, right):
    high, low = parts(left)
    right_high, right_low = parts(right)
    return dot_t(
        jnp.concatenate([high, low, high], axis=1),
        jnp.concatenate([right_high, right_high, right_low], axis=1),
    )


def dot_t(left, right):
    return lax.dot_general(left, right, (((1,), (1,)), ((), ())), preferred_element_type=f32)


def sigmoid(values):
    return 1.0 / (1.0 + jnp.exp(-values))


def silu(values):
    return values * sigmoid(values)


def softplus(values):
    return jnp.maximum(values, 0.0) + jnp.log1p(jnp.exp(-jnp.abs(values)))


def unit(values):
    return values * lax.rsqrt(jnp.sum(values * values, axis=-1, keepdims=True) + 1e-06)


def square_iotas():
    rows = lax.broadcasted_iota(jnp.int32, (T, T), 0)
    columns = lax.broadcasted_iota(jnp.int32, (T, T), 1)
    return rows, columns


def upper_inverses(uppers):
    rows, columns = square_iotas()
    identity = (rows == columns).astype(f32)
    inside = (rows >> 3) == (columns >> 3)
    small = [jnp.where(inside, u, 0.0) for u in uppers]
    squares = [mm(n, n) for n in small]
    stacked = [mm(jnp.concatenate([s, n], axis=0), s) for s, n in zip(squares, small)]
    firsts = [identity - n + s - z[T:] for n, s, z in zip(small, squares, stacked)]
    result = [p + mm(p, z[:T]) for p, z in zip(firsts, stacked)]
    upper_lefts = [left_parts(u) for u in uppers]
    rows, columns = jnp.concatenate([rows, rows], axis=1), jnp.concatenate([columns, columns], axis=1)
    for shift in (3, 4, 5, 6):
        off = ((rows >> (shift + 1)) == (columns >> (shift + 1))) & (
            (rows >> shift) != (columns >> shift)
        )
        off = off.astype(f32).astype(bf16)
        lefts = [left_parts(w) for w in result]
        rights = [right_parts(w) for w in result]
        middles = [mm_parts(off * u, r) for u, r in zip(upper_lefts, rights)]
        result = [
            w - mm_parts(left, right_parts(m)) for w, left, m in zip(result, lefts, middles)
        ]
    return result


def masks_kernel(core_ref, out_ref):
    rows, columns = square_iotas()
    out_ref[0] = (rows <= columns).astype(f32)
    out_ref[1] = (rows == columns).astype(f32)


def column_of(row_ref):
    rows = lax.broadcasted_iota(jnp.int32, (VH, VH), 0)
    columns = lax.broadcasted_iota(jnp.int32, (VH, VH), 1)
    return jnp.sum(jnp.where(rows == columns, row_ref[...], 0.0), axis=1, keepdims=True)


def norm_kernel(
    core_ref,
    mask_ref,
    x_ref,
    gain_ref,
    wb_ref,
    wd_ref,
    rate_ref,
    dtb_ref,
    bb_ref,
    normed_ref,
    bt_ref,
    rt_ref,
    rb_ref,
):
    x = x_ref[...]
    mean_square = jnp.mean(x * x, axis=-1, keepdims=True)
    normed = (x * lax.rsqrt(mean_square + 1e-06) * gain_ref[...]).astype(bf16)
    normed_ref[...] = normed
    bt_ref[...] = sigmoid(dot_t(wb_ref[...], normed) + column_of(bb_ref))
    log_decay = -jnp.exp(column_of(rate_ref)) * softplus(
        dot_t(wd_ref[...], normed) + column_of(dtb_ref)
    )
    running = jnp.dot(log_decay, mask_ref[0], precision=HIGHEST, preferred_element_type=f32)
    rt_ref[...] = running
    for h in range(VH):
        rb_ref[h] = jnp.broadcast_to(running[h : h + 1], (T, T)).T


def inverses_kernel(
    core_ref, normed_ref, bt_ref, rt_ref, rb_ref, wk_ref, keys_ref, kt_ref, inverse_ref
):
    rows, columns = square_iotas()
    key_all = silu(jnp.dot(normed_ref[...], wk_ref[...], preferred_element_type=f32))
    keys = [unit(key_all[:, i * DK : (i + 1) * DK]) for i in range(KH)]
    keys_t = [k.T for k in keys]
    for i in range(KH):
        keys_ref[i] = keys[i]
        kt_ref[i] = keys_t[i]
    grams = [mm(k, kt) for k, kt in zip(keys, keys_t)]
    strict = rows < columns
    uppers = []
    for h in range(VH):
        spread = jnp.minimum(rt_ref[h : h + 1] - rb_ref[h], 0.0)
        uppers.append(jnp.where(strict, bt_ref[h : h + 1] * jnp.exp(spread) * grams[h // 2], 0.0))
    for h, inverse in enumerate(upper_inverses(uppers)):
        inverse_ref[h] = inverse


def maps_kernel(
    core_ref,
    mask_ref,
    normed_ref,
    bt_ref,
    rt_ref,
    wv_ref,
    keys_ref,
    kt_ref,
    inverse_ref,
    send_ref,
    own_ref,
    yt_ref,
):
    value_all = silu(jnp.dot(normed_ref[...], wv_ref[...], preferred_element_type=f32))
    other_rows = pl.ds(pl.multiple_of((1 - core_ref[0]) * HALF, HALF), HALF)
    for i in range(KH):
        key_right = right_parts(keys_ref[i])
        for h in (2 * i, 2 * i + 1):
            r_row, b_row = rt_ref[h : h + 1], bt_ref[h : h + 1]
            value_t = value_all[:, h * DV : (h + 1) * DV].T
            right_t = jnp.concatenate(
                [b_row * value_t, (b_row * jnp.exp(r_row)) * kt_ref[i]], axis=0
            )
            solved = mm(right_t, inverse_ref[h])
            yt_ref[h] = solved
            end = r_row[:, T - 1 : T]
            both = mm_parts(left_parts(solved * jnp.exp(end - r_row)), key_right)
            own_ref[h] = both[:DV]
            send_ref[h, 0:DK] = jnp.exp(end) * mask_ref[1] - both[DV:]
            send_ref[h, DK : DK + HALF] = own_ref[h, other_rows, :]


def readers_kernel(
    normed_ref, wq_hbm, kt_ref, yt_ref, rt_ref, rb_ref, local_ref, reader_ref, wq_s, sem
):
    copy = pltpu.make_async_copy(wq_hbm, wq_s, sem)
    copy.start()
    rows, columns = square_iotas()
    inclusive = rows >= columns
    copy.wait()
    query_all = silu(jnp.dot(normed_ref[...], wq_s[...], preferred_element_type=f32))
    for i in range(KH):
        query = unit(query_all[:, i * DK : (i + 1) * DK]) * DK ** (-0.5)
        product = mm(query, kt_ref[i])
        for h in (2 * i, 2 * i + 1):
            spread = jnp.minimum(rb_ref[h] - rt_ref[h : h + 1], 0.0)
            both = mm_t(jnp.where(inclusive, jnp.exp(spread) * product, 0.0), yt_ref[h])
            local_ref[h] = both[:, :DV]
            reader_ref[h] = jnp.exp(rb_ref[h]) * query - both[:, DV:]


def make_readers(normed, wq, *arguments):
    vmem = pl.BlockSpec(memory_space=pltpu.VMEM)
    return pl.pallas_call(
        readers_kernel,
        in_specs=[vmem, pl.BlockSpec(memory_space=pltpu.HBM)] + [vmem] * len(arguments),
        out_specs=[vmem, vmem],
        out_shape=[jax.ShapeDtypeStruct((VH, T, T), f32)] * 2,
        scratch_shapes=[pltpu.VMEM(wq.shape, wq.dtype), pltpu.SemaphoreType.DMA],
        compiler_params=pltpu.CompilerParams(vmem_limit_bytes=8 * MIB),
        cost_estimate=pl.CostEstimate(
            flops=2 * 10**9, bytes_accessed=8 * 2**20, transcendentals=10**6
        ),
        name="readers",
    )(normed, wq, *arguments)


def on_each_core(core_ref, body):
    for core in (0, 1):

        @pl.when(core_ref[0] == core)
        def _(core=core):
            body(core)


def initial_kernel(place_ref, carry_ref, out_ref):
    state = carry_ref[place_ref[0]].T

    @pl.when(place_ref[1] == 0)
    def _():
        out_ref[...] = state[:HALF]

    @pl.when(place_ref[1] == 1)
    def _():
        out_ref[...] = state[HALF:]


def compose_kernel(core_ref, sent_ref, own_ref, got_ref, out_ref):

    def body(core):
        mine = slice(core * HALF, core * HALF + HALF)
        for h in range(VH):
            own_b, got_b = own_ref[h, mine], got_ref[h, DK : DK + HALF]
            if core == 0:
                first_a, first_b, second_a, second_b = sent_ref, own_b, got_ref, got_b
            else:
                first_a, first_b, second_a, second_b = got_ref, got_b, sent_ref, own_b
            both = mm(jnp.concatenate([first_a[h, mine], first_b], axis=0), second_a[h, 0:DK])
            out_ref[h, 0:HALF] = both[:HALF]
            out_ref[h, HALF : 2 * HALF] = both[HALF:] + second_b

    on_each_core(core_ref, body)


def scan_kernel(core_ref, map_ref, other_ref, initial_ref, out_ref):

    def body(core):
        current = initial_ref[...]
        count = map_ref.shape[0]
        for p in range(count):
            out_ref[p] = current
            if p < count - 1:
                halves = [map_ref[p, 0:HALF], other_ref[p]]
                right = jnp.concatenate(halves if core == 0 else halves[::-1], axis=0)
                current = mm(current, right) + map_ref[p, HALF : 2 * HALF]

    on_each_core(core_ref, body)


def enter_kernel(core_ref, state_ref, sent_ref, own_ref, got_ref, keep_ref, send_ref):

    def body(core):
        given, moved = (keep_ref, send_ref) if core == 0 else (send_ref, keep_ref)
        for h in range(VH):
            state = state_ref[h]
            given[h] = state
            if core == 0:
                moved[h] = mm(state, sent_ref[h, 0:DK]) + own_ref[h, 0:HALF]
            else:
                moved[h] = mm(state, got_ref[h, 0:DK]) + got_ref[h, DK : DK + HALF]

    on_each_core(core_ref, body)


def entering_of(core_ref, keep_ref, got_ref, h):
    keep, got = keep_ref[h], got_ref[h]
    first = core_ref[0] == 0
    return jnp.concatenate([jnp.where(first, keep, got), jnp.where(first, got, keep)], axis=0)


def output_kernel(
    core_ref, keep_ref, got_ref, local_ref, reader_ref, gain_ref, x_ref, wo_ref, out_ref, wo_s, sem
):
    copy = pltpu.make_async_copy(wo_ref, wo_s, sem)
    copy.start()
    heads = []
    for h in range(VH):
        entering = entering_of(core_ref, keep_ref, got_ref, h)
        core = local_ref[h] + mm_t(reader_ref[h], entering)
        mean_square = jnp.mean(core * core, axis=-1, keepdims=True)
        heads.append((core * lax.rsqrt(mean_square + 1e-06) * gain_ref[...]).astype(bf16))
    copy.wait()
    out_ref[...] = x_ref[...] + jnp.dot(
        jnp.concatenate(heads, axis=1), wo_s[...], preferred_element_type=f32
    )


def boundary_kernel(core_ref, keep_ref, got_ref, sent_ref, own_ref, out_ref):
    for h in range(VH):
        entering = entering_of(core_ref, keep_ref, got_ref, h)
        out_ref[h] = (mm(entering, sent_ref[h, 0:DK]) + own_ref[h]).T


def plain_call(kernel, name, outputs, flops, bytes_accessed, arguments, in_hbm=(), scratch=(), limit=6 * MIB):
    vmem = pl.BlockSpec(memory_space=pltpu.VMEM)
    specs = [pl.BlockSpec(memory_space=pltpu.SMEM)] + [
        pl.BlockSpec(memory_space=pl.ANY) if i in in_hbm else vmem
        for i in range(1, len(arguments))
    ]
    several = isinstance(outputs, list)
    return pl.pallas_call(
        kernel,
        in_specs=specs,
        out_specs=[vmem] * len(outputs) if several else vmem,
        out_shape=outputs,
        scratch_shapes=scratch,
        compiler_params=pltpu.CompilerParams(vmem_limit_bytes=limit),
        cost_estimate=pl.CostEstimate(
            flops=flops, bytes_accessed=bytes_accessed, transcendentals=0
        ),
        name=name,
    )(*arguments)


def on_device(
    stream,
    norm_gain,
    w_query,
    w_key,
    w_value,
    w_beta,
    w_decay,
    a_log,
    dt_bias,
    beta_bias,
    head_gain,
    w_output,
    carry_state,
):
    count = lax.axis_size("seq")
    position = lax.axis_index("seq")
    core = (position % 2).astype(jnp.int32)[None]
    chips = count // 2
    pairs = [(i, i ^ 1) for i in range(count)]
    groups = [[2 * i + c for i in range(chips)] for c in range(2)]
    x = stream[0]
    shape = lambda *dims: jax.ShapeDtypeStruct(dims, f32)

    masks = plain_call(masks_kernel, "masks", shape(2, T, T), 10**11, 200 * 2**20, (core,))
    normed, bt, rt, rb = plain_call(
        norm_kernel,
        "norm_and_gates",
        [jax.ShapeDtypeStruct(x.shape, bf16), shape(VH, T), shape(VH, T), shape(VH, T, T)],
        10**9,
        100 * 2**20,
        (
            core,
            masks,
            x,
            norm_gain,
            w_beta[0].T,
            w_decay[0].T,
            a_log,
            dt_bias,
            beta_bias,
        ),
    )
    place = jnp.stack([position // 2, position % 2]).astype(jnp.int32)
    place, normed = lax.optimization_barrier((place, normed))
    initial = plain_call(
        initial_kernel, "initial_state", shape(HALF, DK), 10**6, 2**20, (place, carry_state[0])
    )
    keys, kt, inverses = plain_call(
        inverses_kernel,
        "inverses",
        [shape(KH, T, DK), shape(KH, DK, T), shape(VH, T, T)],
        2 * 10**9,
        20 * 2**20,
        (core, normed, bt, rt, rb, w_key[0]),
        limit=20 * MIB,
    )
    maps, drives, yt = plain_call(
        maps_kernel,
        "block_maps",
        [shape(VH, DK + HALF, DK), shape(VH, DV, DK), shape(VH, DK + DV, T)],
        2 * 10**9,
        10 * 2**20,
        (core, masks, normed, bt, rt, w_value[0], keys, kt, inverses),
        limit=10 * MIB,
    )
    maps_other = lax.ppermute(maps, "seq", pairs)
    local, reader = make_readers(normed, w_query[0], kt, yt, rt, rb)
    maps_other, local, reader = lax.optimization_barrier((maps_other, local, reader))

    chip_maps = plain_call(
        compose_kernel,
        "compose",
        shape(VH, 2 * HALF, DK),
        10**9,
        5 * 2**20,
        (core, maps, drives, maps_other),
    )
    gathered = lax.all_to_all(chip_maps, "seq", 0, 0, axis_index_groups=groups)
    gathered_other = lax.ppermute(gathered[:, :HALF], "seq", pairs)
    states = plain_call(
        scan_kernel,
        "scan_chips",
        shape(chips, HALF, DK),
        10**8,
        30 * 2**20,
        (core, gathered, gathered_other, initial),
    )
    returned = lax.all_to_all(states, "seq", 0, 0, axis_index_groups=groups)
    keep, send = plain_call(
        enter_kernel,
        "enter",
        [shape(VH, HALF, DK)] * 2,
        10**9,
        30 * 2**20,
        (core, returned, maps, drives, maps_other),
    )
    got = lax.ppermute(send, "seq", pairs)
    rows_out = plain_call(
        output_kernel,
        "output_rows",
        shape(*x.shape),
        3 * 10**9,
        8 * 2**20,
        (core, keep, got, local, reader, head_gain, x, w_output[0]),
        in_hbm=(7,),
        scratch=[pltpu.VMEM(w_output.shape[1:], bf16), pltpu.SemaphoreType.DMA],
    )
    sections = lax.axis_size("section")
    onward = [(i, (i + 1) % sections) for i in range(sections)]
    chunk = T // CHUNKS
    next_rows = jnp.concatenate(
        [lax.ppermute(rows_out[i * chunk : (i + 1) * chunk], "section", onward) for i in range(CHUNKS)]
    )
    boundary = plain_call(
        boundary_kernel, "boundary", shape(VH, DK, DV), 10**9, 4 * 2**20, (core, keep, got, maps, drives)
    )
    return (next_rows[None], boundary[None, None])


def solution(mesh):
    placed = (
        P("section", "seq", None),
        P("section", None),
        P("section", None, None),
        P("section", None, None),
        P("section", None, None),
        P("section", None, None),
        P("section", None, None),
        P("section", None),
        P("section", None),
        P("section", None),
        P("section", None),
        P("section", None, None),
        P("section", None, None, None),
    )
    return jax.shard_map(
        on_device,
        mesh=mesh,
        in_specs=placed,
        out_specs=(P("section", "seq", None), P("section", "seq", None, None, None)),
        check_vma=False,
    )
```

```python
import functools

import jax
import jax.numpy as jnp
from jax import lax
from jax.experimental import pallas as pl
from jax.experimental.pallas import tpu as pltpu
from jax.sharding import PartitionSpec as P

KH = 8
VH = 16
DK = 128
DV = 128
T = 128
HALF = 64
CHUNKS = 4
PARTS = 1
SPLIT = 2
f32 = jnp.float32
bf16 = jnp.bfloat16
HIGHEST = lax.Precision.HIGHEST
MIB = 2**20
BATCH = 4


def parts(values):
    high = values.astype(bf16)
    return high, (values - high.astype(f32)).astype(bf16)


def left_parts(values):
    return jnp.concatenate(parts(values), axis=1)


def right_parts(values):
    both = jnp.concatenate(parts(values), axis=1)
    return jnp.concatenate([both, both], axis=0)


def mm_parts(left, right):
    both = jnp.dot(left, right, preferred_element_type=f32)
    columns = both.shape[1] // 2
    return both[:, :columns] + both[:, columns:]


def mm(left, right):
    return mm_parts(left_parts(left), right_parts(right))


def mm_t(left, right):
    high, low = parts(left)
    right_high, right_low = parts(right)
    return dot_t(
        jnp.concatenate([high, low, high], axis=1),
        jnp.concatenate([right_high, right_high, right_low], axis=1),
    )


def dot_t(left, right):
    return lax.dot_general(left, right, (((1,), (1,)), ((), ())), preferred_element_type=f32)


def sigmoid(values):
    return 1.0 / (1.0 + jnp.exp(-values))


def silu(values):
    return values * sigmoid(values)


def softplus(values):
    return jnp.maximum(values, 0.0) + jnp.log1p(jnp.exp(-jnp.abs(values)))


def unit(values):
    return values * lax.rsqrt(jnp.sum(values * values, axis=-1, keepdims=True) + 1e-06)


def square_iotas():
    rows = lax.broadcasted_iota(jnp.int32, (T, T), 0)
    columns = lax.broadcasted_iota(jnp.int32, (T, T), 1)
    return rows, columns


def upper_inverses(uppers):
    rows, columns = square_iotas()
    identity = (rows == columns).astype(f32)
    inside = (rows >> 3) == (columns >> 3)
    small = [jnp.where(inside, u, 0.0) for u in uppers]
    squares = [mm(n, n) for n in small]
    stacked = [mm(jnp.concatenate([s, n], axis=0), s) for s, n in zip(squares, small)]
    firsts = [identity - n + s - z[T:] for n, s, z in zip(small, squares, stacked)]
    result = [p + mm(p, z[:T]) for p, z in zip(firsts, stacked)]
    upper_lefts = [left_parts(u) for u in uppers]
    rows, columns = jnp.concatenate([rows, rows], axis=1), jnp.concatenate([columns, columns], axis=1)
    for shift in (3, 4, 5, 6):
        off = ((rows >> (shift + 1)) == (columns >> (shift + 1))) & (
            (rows >> shift) != (columns >> shift)
        )
        off = off.astype(f32).astype(bf16)
        lefts = [left_parts(w) for w in result]
        rights = [right_parts(w) for w in result]
        middles = [mm_parts(off * u, r) for u, r in zip(upper_lefts, rights)]
        result = [
            w - mm_parts(left, right_parts(m)) for w, left, m in zip(result, lefts, middles)
        ]
    return result


def masks_kernel(core_ref, out_ref):
    rows, columns = square_iotas()
    out_ref[0] = (rows <= columns).astype(f32)
    out_ref[1] = (rows == columns).astype(f32)


def column_of(row_ref):
    rows = lax.broadcasted_iota(jnp.int32, (VH, VH), 0)
    columns = lax.broadcasted_iota(jnp.int32, (VH, VH), 1)
    return jnp.sum(jnp.where(rows == columns, row_ref[...], 0.0), axis=1, keepdims=True)


def norm_kernel(
    core_ref,
    mask_ref,
    x_ref,
    gain_ref,
    wb_ref,
    wd_ref,
    rate_ref,
    dtb_ref,
    bb_ref,
    normed_ref,
    bt_ref,
    rt_ref,
    rb_ref,
):
    x = x_ref[...]
    mean_square = jnp.mean(x * x, axis=-1, keepdims=True)
    normed = (x * lax.rsqrt(mean_square + 1e-06) * gain_ref[...]).astype(bf16)
    normed_ref[...] = normed
    bt_ref[...] = sigmoid(dot_t(wb_ref[...], normed) + column_of(bb_ref))
    log_decay = -jnp.exp(column_of(rate_ref)) * softplus(
        dot_t(wd_ref[...], normed) + column_of(dtb_ref)
    )
    running = jnp.dot(log_decay, mask_ref[0], precision=HIGHEST, preferred_element_type=f32)
    rt_ref[...] = running
    for h in range(VH):
        rb_ref[h] = jnp.broadcast_to(running[h : h + 1], (T, T)).T


def inverses_kernel(
    core_ref, normed_ref, bt_ref, rt_ref, rb_ref, wk_ref, keys_ref, kt_ref, inverse_ref
):
    rows, columns = square_iotas()
    key_all = silu(jnp.dot(normed_ref[...], wk_ref[...], preferred_element_type=f32))
    keys = [unit(key_all[:, i * DK : (i + 1) * DK]) for i in range(KH)]
    keys_t = [k.T for k in keys]
    for i in range(KH):
        keys_ref[i] = keys[i]
        kt_ref[i] = keys_t[i]
    grams = [mm(k, kt) for k, kt in zip(keys, keys_t)]
    strict = rows < columns
    uppers = []
    for h in range(VH):
        spread = jnp.minimum(rt_ref[h : h + 1] - rb_ref[h], 0.0)
        uppers.append(jnp.where(strict, bt_ref[h : h + 1] * jnp.exp(spread) * grams[h // 2], 0.0))
    for h, inverse in enumerate(upper_inverses(uppers)):
        inverse_ref[h] = inverse


def maps_kernel(
    part,
    core_ref,
    mask_ref,
    normed_ref,
    bt_ref,
    rt_ref,
    wv_ref,
    keys_ref,
    kt_ref,
    inverse_ref,
    send_ref,
    own_ref,
    yt_ref,
):
    span = VH // SPLIT
    columns = slice(part * span * DV, (part + 1) * span * DV)
    value_all = silu(jnp.dot(normed_ref[...], wv_ref[:, columns], preferred_element_type=f32))
    other_rows = pl.ds(pl.multiple_of((1 - core_ref[0]) * HALF, HALF), HALF)
    for n in range(span):
        h = part * span + n
        i = h // 2
        key_right = right_parts(keys_ref[i])
        r_row, b_row = rt_ref[h : h + 1], bt_ref[h : h + 1]
        value_t = value_all[:, n * DV : (n + 1) * DV].T
        right_t = jnp.concatenate([b_row * value_t, (b_row * jnp.exp(r_row)) * kt_ref[i]], axis=0)
        solved = mm(right_t, inverse_ref[h])
        yt_ref[n] = solved
        end = r_row[:, T - 1 : T]
        both = mm_parts(left_parts(solved * jnp.exp(end - r_row)), key_right)
        own_ref[n] = both[:DV]
        send_ref[n, 0:DK] = jnp.exp(end) * mask_ref[1] - both[DV:]
        send_ref[n, DK : DK + HALF] = own_ref[n, other_rows, :]


def of_head(refs, h):
    span = VH // len(refs)
    return refs[h // span].at[h % span]


def readers_kernel(
    normed_ref, wq_ref, kt_ref, rt_ref, rb_ref, *refs
):
    yt_refs, (local_ref, reader_ref) = refs[:SPLIT], refs[SPLIT:]
    rows, columns = square_iotas()
    inclusive = rows >= columns
    query_all = silu(jnp.dot(normed_ref[...], wq_ref[...], preferred_element_type=f32))
    for i in range(KH):
        query = unit(query_all[:, i * DK : (i + 1) * DK]) * DK ** (-0.5)
        product = mm(query, kt_ref[i])
        for h in (2 * i, 2 * i + 1):
            spread = jnp.minimum(rb_ref[h] - rt_ref[h : h + 1], 0.0)
            both = mm_t(jnp.where(inclusive, jnp.exp(spread) * product, 0.0), of_head(yt_refs, h)[...])
            local_ref[h] = both[:, :DV]
            reader_ref[h] = jnp.exp(rb_ref[h]) * query - both[:, DV:]


def make_readers(normed, wq, *arguments):
    vmem = pl.BlockSpec(memory_space=pltpu.VMEM)
    return pl.pallas_call(
        readers_kernel,
        in_specs=[vmem] * (2 + len(arguments)),
        out_specs=[vmem, vmem],
        out_shape=[jax.ShapeDtypeStruct((VH, T, T), f32)] * 2,
        compiler_params=pltpu.CompilerParams(vmem_limit_bytes=8 * MIB),
        cost_estimate=pl.CostEstimate(
            flops=2 * 10**9, bytes_accessed=8 * 2**20, transcendentals=10**6
        ),
        name="readers",
    )(normed, wq, *arguments)


def on_each_core(core_ref, body):
    for core in (0, 1):

        @pl.when(core_ref[0] == core)
        def _(core=core):
            body(core)


def initial_kernel(place_ref, carry_ref, out_ref):
    state = carry_ref[place_ref[0]].T

    @pl.when(place_ref[1] == 0)
    def _():
        out_ref[...] = state[:HALF]

    @pl.when(place_ref[1] == 1)
    def _():
        out_ref[...] = state[HALF:]


def compose_kernel(core_ref, *refs):
    sent_refs, own_refs, got_refs = (refs[n * SPLIT : (n + 1) * SPLIT] for n in range(3))
    out_ref = refs[-1]

    def body(core):
        mine = slice(core * HALF, core * HALF + HALF)
        for h in range(VH):
            sent, own, got = (of_head(r, h) for r in (sent_refs, own_refs, got_refs))
            own_b, got_b = own[mine], got[DK : DK + HALF]
            if core == 0:
                first_a, first_b, second_a, second_b = sent, own_b, got, got_b
            else:
                first_a, first_b, second_a, second_b = got, got_b, sent, own_b
            both = mm(jnp.concatenate([first_a[mine], first_b], axis=0), second_a[0:DK])
            out_ref[h, 0:HALF] = both[:HALF]
            out_ref[h, HALF : 2 * HALF] = both[HALF:] + second_b

    on_each_core(core_ref, body)


def scan_kernel(core_ref, map_ref, other_ref, initial_ref, out_ref):

    def body(core):
        count = map_ref.shape[0]

        def full(p):
            halves = [map_ref[p, 0:HALF], other_ref[p]]
            return jnp.concatenate(halves if core == 0 else halves[::-1], axis=0)

        drive = lambda p: map_ref[p, HALF : 2 * HALF]
        pairs = []
        for p in range(0, count - 2, 2):
            both = mm(jnp.concatenate([full(p), drive(p)], axis=0), full(p + 1))
            pairs.append((both[:DK], both[DK:] + drive(p + 1)))
        current = initial_ref[...]
        for p in range(0, count, 2):
            out_ref[p] = current
            out_ref[p + 1] = mm(current, full(p)) + drive(p)
            if p < count - 2:
                current = mm(current, pairs[p // 2][0]) + pairs[p // 2][1]

    on_each_core(core_ref, body)


def enter_kernel(core_ref, state_ref, *refs):
    sent_refs, own_refs, got_refs = (refs[n * SPLIT : (n + 1) * SPLIT] for n in range(3))
    keep_ref, send_ref = refs[3 * SPLIT :]

    def body(core):
        given, moved = (keep_ref, send_ref) if core == 0 else (send_ref, keep_ref)
        for h in range(VH):
            sent, own, got = (of_head(r, h) for r in (sent_refs, own_refs, got_refs))
            state = state_ref[h]
            given[h] = state
            if core == 0:
                moved[h] = mm(state, sent[0:DK]) + own[0:HALF]
            else:
                moved[h] = mm(state, got[0:DK]) + got[DK : DK + HALF]

    on_each_core(core_ref, body)


def entering_of(core_ref, keep_ref, got_ref, h):
    keep, got = keep_ref[h], got_ref[h]
    first = core_ref[0] == 0
    return jnp.concatenate([jnp.where(first, keep, got), jnp.where(first, got, keep)], axis=0)


def output_kernel(
    part, core_ref, keep_ref, got_ref, local_ref, reader_ref, gain_ref, x_ref, wo_ref, out_ref
):
    rows = slice(part * T // PARTS, (part + 1) * T // PARTS)
    heads = []
    for h in range(VH):
        entering = entering_of(core_ref, keep_ref, got_ref, h)
        core = local_ref[h, rows] + mm_t(reader_ref[h, rows], entering)
        mean_square = jnp.mean(core * core, axis=-1, keepdims=True)
        heads.append((core * lax.rsqrt(mean_square + 1e-06) * gain_ref[...]).astype(bf16))
    out_ref[...] = x_ref[rows] + jnp.dot(
        jnp.concatenate(heads, axis=1), wo_ref[...], preferred_element_type=f32
    )


def boundary_kernel(core_ref, keep_ref, got_ref, *refs):
    sent_refs, own_refs, out_ref = refs[:SPLIT], refs[SPLIT : 2 * SPLIT], refs[-1]
    for h in range(VH):
        entering = entering_of(core_ref, keep_ref, got_ref, h)
        sent, own = of_head(sent_refs, h), of_head(own_refs, h)
        out_ref[h] = (mm(entering, sent[0:DK]) + own[...]).T


def plain_call(kernel, name, outputs, flops, bytes_accessed, arguments, limit=6 * MIB):
    vmem = pl.BlockSpec(memory_space=pltpu.VMEM)
    specs = [pl.BlockSpec(memory_space=pltpu.SMEM)] + [vmem] * (len(arguments) - 1)
    several = isinstance(outputs, list)
    return pl.pallas_call(
        kernel,
        in_specs=specs,
        out_specs=[vmem] * len(outputs) if several else vmem,
        out_shape=outputs,
        compiler_params=pltpu.CompilerParams(vmem_limit_bytes=limit),
        cost_estimate=pl.CostEstimate(
            flops=flops, bytes_accessed=bytes_accessed, transcendentals=0
        ),
        name=name,
    )(*arguments)


def on_device(
    stream,
    norm_gain,
    w_query,
    w_key,
    w_value,
    w_beta,
    w_decay,
    a_log,
    dt_bias,
    beta_bias,
    head_gain,
    w_output,
    carry_state,
):
    count = lax.axis_size("seq")
    position = lax.axis_index("seq")
    core = (position % 2).astype(jnp.int32)[None]
    chips = count // 2
    pairs = [(i, i ^ 1) for i in range(count)]
    groups = [[2 * i + c for i in range(chips)] for c in range(2)]
    x = stream[0]
    shape = lambda *dims: jax.ShapeDtypeStruct(dims, f32)

    masks = plain_call(masks_kernel, "masks", shape(2, T, T), 10**11, 200 * 2**20, (core,))
    normed, bt, rt, rb = plain_call(
        norm_kernel,
        "norm_and_gates",
        [jax.ShapeDtypeStruct(x.shape, bf16), shape(VH, T), shape(VH, T), shape(VH, T, T)],
        10**9,
        100 * 2**20,
        (
            core,
            masks,
            x,
            norm_gain,
            w_beta[0].T,
            w_decay[0].T,
            a_log,
            dt_bias,
            beta_bias,
        ),
    )
    place = jnp.stack([position // 2, position % 2]).astype(jnp.int32)
    place, normed = lax.optimization_barrier((place, normed))
    initial = plain_call(
        initial_kernel, "initial_state", shape(HALF, DK), 10**6, 2**20, (place, carry_state[0])
    )
    keys, kt, inverses = plain_call(
        inverses_kernel,
        "inverses",
        [shape(KH, T, DK), shape(KH, DK, T), shape(VH, T, T)],
        2 * 10**9,
        20 * 2**20,
        (core, normed, bt, rt, rb, w_key[0]),
        limit=20 * MIB,
    )
    span = VH // SPLIT
    maps, drives, solved, maps_other = [], [], [], []
    for part in range(SPLIT):
        sent, own, yt = plain_call(
            functools.partial(maps_kernel, part),
            "block_maps",
            [shape(span, DK + HALF, DK), shape(span, DV, DK), shape(span, DK + DV, T)],
            2 * 10**9,
            10 * 2**20,
            (core, masks, normed, bt, rt, w_value[0], keys, kt, inverses),
            limit=10 * MIB,
        )
        maps.append(sent)
        drives.append(own)
        solved.append(yt)
        maps_other.append(lax.ppermute(sent, "seq", pairs))
    local, reader = make_readers(normed, w_query[0], kt, rt, rb, *solved)
    maps_other, local, reader = lax.optimization_barrier((maps_other, local, reader))

    chip_maps = plain_call(
        compose_kernel,
        "compose",
        shape(VH, 2 * HALF, DK),
        10**9,
        5 * 2**20,
        (core, *maps, *drives, *maps_other),
    )
    gathered = lax.all_to_all(chip_maps, "seq", 0, 0, axis_index_groups=groups)
    gathered_other = lax.ppermute(gathered[:, :HALF], "seq", pairs)
    states = plain_call(
        scan_kernel,
        "scan_chips",
        shape(chips, HALF, DK),
        10**8,
        30 * 2**20,
        (core, gathered, gathered_other, initial),
    )
    returned = lax.all_to_all(states, "seq", 0, 0, axis_index_groups=groups)
    keep, send = plain_call(
        enter_kernel,
        "enter",
        [shape(VH, HALF, DK)] * 2,
        10**9,
        30 * 2**20,
        (core, returned, *maps, *drives, *maps_other),
    )
    got = lax.ppermute(send, "seq", pairs)
    sections = lax.axis_size("section")
    onward = [(i, (i + 1) % sections) for i in range(sections)]
    chunk = T // CHUNKS
    arrived = []
    for part in range(PARTS):
        rows_out = plain_call(
            functools.partial(output_kernel, part),
            "output_rows",
            shape(T // PARTS, x.shape[1]),
            10**9,
            8 * 2**20,
            (core, keep, got, local, reader, head_gain, x, w_output[0]),
        )
        for i in range(0, T // PARTS, chunk):
            arrived.append(lax.ppermute(rows_out[i : i + chunk], "section", onward))
    next_rows = jnp.concatenate(arrived)
    boundary = plain_call(
        boundary_kernel, "boundary", shape(VH, DK, DV), 10**9, 4 * 2**20, (core, keep, got, *maps, *drives)
    )
    return (next_rows[None], boundary[None, None])


def solution(mesh):
    placed = (
        P("section", "seq", None),
        P("section", None),
        P("section", None, None),
        P("section", None, None),
        P("section", None, None),
        P("section", None, None),
        P("section", None, None),
        P("section", None),
        P("section", None),
        P("section", None),
        P("section", None),
        P("section", None, None),
        P("section", None, None, None),
    )
    return jax.shard_map(
        on_device,
        mesh=mesh,
        in_specs=placed,
        out_specs=(P("section", "seq", None), P("section", "seq", None, None, None)),
        check_vma=False,
    )
```

```python
import functools

import jax
import jax.numpy as jnp
from jax import lax
from jax.experimental import pallas as pl
from jax.experimental.pallas import tpu as pltpu
from jax.sharding import PartitionSpec as P

KH = 8
VH = 16
DK = 128
DV = 128
T = 128
HALF = 64
CHUNKS = 4
PARTS = 1
SPLIT = 2
f32 = jnp.float32
bf16 = jnp.bfloat16
HIGHEST = lax.Precision.HIGHEST
MIB = 2**20
BATCH = 4


def parts(values):
    high = values.astype(bf16)
    return high, (values - high.astype(f32)).astype(bf16)


def left_parts(values):
    return jnp.concatenate(parts(values), axis=1)


def right_parts(values):
    both = jnp.concatenate(parts(values), axis=1)
    return jnp.concatenate([both, both], axis=0)


def mm_parts(left, right):
    both = jnp.dot(left, right, preferred_element_type=f32)
    columns = both.shape[1] // 2
    return both[:, :columns] + both[:, columns:]


def mm(left, right):
    return mm_parts(left_parts(left), right_parts(right))


def mm_t(left, right):
    high, low = parts(left)
    right_high, right_low = parts(right)
    return dot_t(
        jnp.concatenate([high, low, high], axis=1),
        jnp.concatenate([right_high, right_high, right_low], axis=1),
    )


def dot_t(left, right):
    return lax.dot_general(left, right, (((1,), (1,)), ((), ())), preferred_element_type=f32)


def sigmoid(values):
    return 1.0 / (1.0 + jnp.exp(-values))


def silu(values):
    return values * sigmoid(values)


def softplus(values):
    return jnp.maximum(values, 0.0) + jnp.log1p(jnp.exp(-jnp.abs(values)))


def unit(values):
    return values * lax.rsqrt(jnp.sum(values * values, axis=-1, keepdims=True) + 1e-06)


def square_iotas():
    rows = lax.broadcasted_iota(jnp.int32, (T, T), 0)
    columns = lax.broadcasted_iota(jnp.int32, (T, T), 1)
    return rows, columns


def upper_inverses(uppers):
    rows, columns = square_iotas()
    identity = (rows == columns).astype(f32)
    inside = (rows >> 3) == (columns >> 3)
    small = [jnp.where(inside, u, 0.0) for u in uppers]
    squares = [mm(n, n) for n in small]
    stacked = [mm(jnp.concatenate([s, n], axis=0), s) for s, n in zip(squares, small)]
    firsts = [identity - n + s - z[T:] for n, s, z in zip(small, squares, stacked)]
    result = [p + mm(p, z[:T]) for p, z in zip(firsts, stacked)]
    upper_lefts = [left_parts(u) for u in uppers]
    rows, columns = jnp.concatenate([rows, rows], axis=1), jnp.concatenate([columns, columns], axis=1)
    for shift in (3, 4, 5, 6):
        off = ((rows >> (shift + 1)) == (columns >> (shift + 1))) & (
            (rows >> shift) != (columns >> shift)
        )
        off = off.astype(f32).astype(bf16)
        lefts = [left_parts(w) for w in result]
        rights = [right_parts(w) for w in result]
        middles = [mm_parts(off * u, r) for u, r in zip(upper_lefts, rights)]
        result = [
            w - mm_parts(left, right_parts(m)) for w, left, m in zip(result, lefts, middles)
        ]
    return result


def masks_kernel(core_ref, out_ref):
    rows, columns = square_iotas()
    out_ref[0] = (rows <= columns).astype(f32)
    out_ref[1] = (rows == columns).astype(f32)


def column_of(row_ref):
    rows = lax.broadcasted_iota(jnp.int32, (VH, VH), 0)
    columns = lax.broadcasted_iota(jnp.int32, (VH, VH), 1)
    return jnp.sum(jnp.where(rows == columns, row_ref[...], 0.0), axis=1, keepdims=True)


def norm_kernel(
    core_ref,
    mask_ref,
    x_ref,
    gain_ref,
    wb_ref,
    wd_ref,
    rate_ref,
    dtb_ref,
    bb_ref,
    normed_ref,
    bt_ref,
    rt_ref,
    rb_ref,
):
    x = x_ref[...]
    mean_square = jnp.mean(x * x, axis=-1, keepdims=True)
    normed = (x * lax.rsqrt(mean_square + 1e-06) * gain_ref[...]).astype(bf16)
    normed_ref[...] = normed
    bt_ref[...] = sigmoid(dot_t(wb_ref[...], normed) + column_of(bb_ref))
    log_decay = -jnp.exp(column_of(rate_ref)) * softplus(
        dot_t(wd_ref[...], normed) + column_of(dtb_ref)
    )
    running = jnp.dot(log_decay, mask_ref[0], precision=HIGHEST, preferred_element_type=f32)
    rt_ref[...] = running
    for h in range(VH):
        rb_ref[h] = jnp.broadcast_to(running[h : h + 1], (T, T)).T


def inverses_kernel(
    core_ref, normed_ref, bt_ref, rt_ref, rb_ref, wk_ref, keys_ref, kt_ref, inverse_ref
):
    rows, columns = square_iotas()
    key_all = silu(jnp.dot(normed_ref[...], wk_ref[...], preferred_element_type=f32))
    keys = [unit(key_all[:, i * DK : (i + 1) * DK]) for i in range(KH)]
    keys_t = [k.T for k in keys]
    for i in range(KH):
        keys_ref[i] = keys[i]
        kt_ref[i] = keys_t[i]
    grams = [mm(k, kt) for k, kt in zip(keys, keys_t)]
    strict = rows < columns
    uppers = []
    for h in range(VH):
        spread = jnp.minimum(rt_ref[h : h + 1] - rb_ref[h], 0.0)
        uppers.append(jnp.where(strict, bt_ref[h : h + 1] * jnp.exp(spread) * grams[h // 2], 0.0))
    for h, inverse in enumerate(upper_inverses(uppers)):
        inverse_ref[h] = inverse


def maps_kernel(
    part,
    core_ref,
    mask_ref,
    normed_ref,
    bt_ref,
    rt_ref,
    wv_ref,
    keys_ref,
    kt_ref,
    inverse_ref,
    send_ref,
    own_ref,
    yt_ref,
):
    span = VH // SPLIT
    columns = slice(part * span * DV, (part + 1) * span * DV)
    value_all = silu(jnp.dot(normed_ref[...], wv_ref[:, columns], preferred_element_type=f32))
    other_rows = pl.ds(pl.multiple_of((1 - core_ref[0]) * HALF, HALF), HALF)
    for n in range(span):
        h = part * span + n
        i = h // 2
        key_right = right_parts(keys_ref[i])
        r_row, b_row = rt_ref[h : h + 1], bt_ref[h : h + 1]
        value_t = value_all[:, n * DV : (n + 1) * DV].T
        right_t = jnp.concatenate([b_row * value_t, (b_row * jnp.exp(r_row)) * kt_ref[i]], axis=0)
        solved = mm(right_t, inverse_ref[h])
        yt_ref[n] = solved
        end = r_row[:, T - 1 : T]
        both = mm_parts(left_parts(solved * jnp.exp(end - r_row)), key_right)
        own_ref[n] = both[:DV]
        send_ref[n, 0:DK] = jnp.exp(end) * mask_ref[1] - both[DV:]
        send_ref[n, DK : DK + HALF] = own_ref[n, other_rows, :]


def of_head(refs, h):
    for ref in refs:
        if h < ref.shape[0]:
            return ref.at[h]
        h -= ref.shape[0]


def readers_kernel(
    keys, normed_ref, wq_ref, kt_ref, rt_ref, rb_ref, *refs
):
    yt_refs, (local_ref, reader_ref) = refs[:SPLIT], refs[SPLIT:]
    columns_of = slice(keys[0] * DK, (keys[-1] + 1) * DK)
    rows, columns = square_iotas()
    inclusive = rows >= columns
    query_all = silu(jnp.dot(normed_ref[...], wq_ref[:, columns_of], preferred_element_type=f32))
    for i, key in enumerate(keys):
        query = unit(query_all[:, i * DK : (i + 1) * DK]) * DK ** (-0.5)
        product = mm(query, kt_ref[key])
        for n in (2 * i, 2 * i + 1):
            h = 2 * key + n % 2
            spread = jnp.minimum(rb_ref[h] - rt_ref[h : h + 1], 0.0)
            both = mm_t(jnp.where(inclusive, jnp.exp(spread) * product, 0.0), of_head(yt_refs, h)[...])
            local_ref[n] = both[:, :DV]
            reader_ref[n] = jnp.exp(rb_ref[h]) * query - both[:, DV:]


def make_readers(keys, *arguments):
    vmem = pl.BlockSpec(memory_space=pltpu.VMEM)
    return pl.pallas_call(
        functools.partial(readers_kernel, keys),
        in_specs=[vmem] * len(arguments),
        out_specs=[vmem, vmem],
        out_shape=[jax.ShapeDtypeStruct((VH // KH * len(keys), T, T), f32)] * 2,
        compiler_params=pltpu.CompilerParams(vmem_limit_bytes=8 * MIB),
        cost_estimate=pl.CostEstimate(
            flops=2 * 10**9, bytes_accessed=8 * 2**20, transcendentals=10**6
        ),
        name="readers",
    )(*arguments)


def on_each_core(core_ref, body):
    for core in (0, 1):

        @pl.when(core_ref[0] == core)
        def _(core=core):
            body(core)


def initial_kernel(place_ref, carry_ref, out_ref):
    state = carry_ref[place_ref[0]].T

    @pl.when(place_ref[1] == 0)
    def _():
        out_ref[...] = state[:HALF]

    @pl.when(place_ref[1] == 1)
    def _():
        out_ref[...] = state[HALF:]


def compose_kernel(core_ref, *refs):
    sent_refs, own_refs, got_refs = (refs[n * SPLIT : (n + 1) * SPLIT] for n in range(3))
    out_ref = refs[-1]

    def body(core):
        mine = slice(core * HALF, core * HALF + HALF)
        for h in range(VH):
            sent, own, got = (of_head(r, h) for r in (sent_refs, own_refs, got_refs))
            own_b, got_b = own[mine], got[DK : DK + HALF]
            if core == 0:
                first_a, first_b, second_a, second_b = sent, own_b, got, got_b
            else:
                first_a, first_b, second_a, second_b = got, got_b, sent, own_b
            both = mm(jnp.concatenate([first_a[mine], first_b], axis=0), second_a[0:DK])
            out_ref[h, 0:HALF] = both[:HALF]
            out_ref[h, HALF : 2 * HALF] = both[HALF:] + second_b

    on_each_core(core_ref, body)


def scan_kernel(core_ref, map_ref, other_ref, initial_ref, out_ref):

    def body(core):
        count = map_ref.shape[0]

        def full(p):
            halves = [map_ref[p, 0:HALF], other_ref[p]]
            return jnp.concatenate(halves if core == 0 else halves[::-1], axis=0)

        drive = lambda p: map_ref[p, HALF : 2 * HALF]
        pairs = []
        for p in range(0, count - 2, 2):
            both = mm(jnp.concatenate([full(p), drive(p)], axis=0), full(p + 1))
            pairs.append((both[:DK], both[DK:] + drive(p + 1)))
        current = initial_ref[...]
        for p in range(0, count, 2):
            out_ref[p] = current
            out_ref[p + 1] = mm(current, full(p)) + drive(p)
            if p < count - 2:
                current = mm(current, pairs[p // 2][0]) + pairs[p // 2][1]

    on_each_core(core_ref, body)


def enter_kernel(core_ref, state_ref, *refs):
    sent_refs, own_refs, got_refs = (refs[n * SPLIT : (n + 1) * SPLIT] for n in range(3))
    keep_ref, send_ref = refs[3 * SPLIT :]

    def body(core):
        given, moved = (keep_ref, send_ref) if core == 0 else (send_ref, keep_ref)
        for h in range(VH):
            sent, own, got = (of_head(r, h) for r in (sent_refs, own_refs, got_refs))
            state = state_ref[h]
            given[h] = state
            if core == 0:
                moved[h] = mm(state, sent[0:DK]) + own[0:HALF]
            else:
                moved[h] = mm(state, got[0:DK]) + got[DK : DK + HALF]

    on_each_core(core_ref, body)


def entering_of(core_ref, keep_ref, got_ref, h):
    keep, got = keep_ref[h], got_ref[h]
    first = core_ref[0] == 0
    return jnp.concatenate([jnp.where(first, keep, got), jnp.where(first, got, keep)], axis=0)


def output_kernel(
    part, core_ref, keep_ref, got_ref, gain_ref, x_ref, wo_ref, *refs
):
    local_refs, reader_refs, out_ref = refs[:2], refs[2:4], refs[-1]
    rows = slice(part * T // PARTS, (part + 1) * T // PARTS)
    heads = []
    for h in range(VH):
        entering = entering_of(core_ref, keep_ref, got_ref, h)
        core = of_head(local_refs, h)[rows] + mm_t(of_head(reader_refs, h)[rows], entering)
        mean_square = jnp.mean(core * core, axis=-1, keepdims=True)
        heads.append((core * lax.rsqrt(mean_square + 1e-06) * gain_ref[...]).astype(bf16))
    out_ref[...] = x_ref[rows] + jnp.dot(
        jnp.concatenate(heads, axis=1), wo_ref[...], preferred_element_type=f32
    )


def boundary_kernel(core_ref, keep_ref, got_ref, *refs):
    sent_refs, own_refs, out_ref = refs[:SPLIT], refs[SPLIT : 2 * SPLIT], refs[-1]
    for h in range(VH):
        entering = entering_of(core_ref, keep_ref, got_ref, h)
        sent, own = of_head(sent_refs, h), of_head(own_refs, h)
        out_ref[h] = (mm(entering, sent[0:DK]) + own[...]).T


def plain_call(kernel, name, outputs, flops, bytes_accessed, arguments, limit=6 * MIB):
    vmem = pl.BlockSpec(memory_space=pltpu.VMEM)
    specs = [pl.BlockSpec(memory_space=pltpu.SMEM)] + [vmem] * (len(arguments) - 1)
    several = isinstance(outputs, list)
    return pl.pallas_call(
        kernel,
        in_specs=specs,
        out_specs=[vmem] * len(outputs) if several else vmem,
        out_shape=outputs,
        compiler_params=pltpu.CompilerParams(vmem_limit_bytes=limit),
        cost_estimate=pl.CostEstimate(
            flops=flops, bytes_accessed=bytes_accessed, transcendentals=0
        ),
        name=name,
    )(*arguments)


def on_device(
    stream,
    norm_gain,
    w_query,
    w_key,
    w_value,
    w_beta,
    w_decay,
    a_log,
    dt_bias,
    beta_bias,
    head_gain,
    w_output,
    carry_state,
):
    count = lax.axis_size("seq")
    position = lax.axis_index("seq")
    core = (position % 2).astype(jnp.int32)[None]
    chips = count // 2
    pairs = [(i, i ^ 1) for i in range(count)]
    groups = [[2 * i + c for i in range(chips)] for c in range(2)]
    x = stream[0]
    shape = lambda *dims: jax.ShapeDtypeStruct(dims, f32)

    masks = plain_call(masks_kernel, "masks", shape(2, T, T), 10**11, 200 * 2**20, (core,))
    normed, bt, rt, rb = plain_call(
        norm_kernel,
        "norm_and_gates",
        [jax.ShapeDtypeStruct(x.shape, bf16), shape(VH, T), shape(VH, T), shape(VH, T, T)],
        10**9,
        100 * 2**20,
        (
            core,
            masks,
            x,
            norm_gain,
            w_beta[0].T,
            w_decay[0].T,
            a_log,
            dt_bias,
            beta_bias,
        ),
    )
    place = jnp.stack([position // 2, position % 2]).astype(jnp.int32)
    place, normed = lax.optimization_barrier((place, normed))
    initial = plain_call(
        initial_kernel, "initial_state", shape(HALF, DK), 10**6, 2**20, (place, carry_state[0])
    )
    keys, kt, inverses = plain_call(
        inverses_kernel,
        "inverses",
        [shape(KH, T, DK), shape(KH, DK, T), shape(VH, T, T)],
        2 * 10**9,
        20 * 2**20,
        (core, normed, bt, rt, rb, w_key[0]),
        limit=20 * MIB,
    )
    span = VH // SPLIT
    maps, drives, solved, maps_other = [], [], [], []
    for part in range(SPLIT):
        sent, own, yt = plain_call(
            functools.partial(maps_kernel, part),
            "block_maps",
            [shape(span, DK + HALF, DK), shape(span, DV, DK), shape(span, DK + DV, T)],
            2 * 10**9,
            10 * 2**20,
            (core, masks, normed, bt, rt, w_value[0], keys, kt, inverses),
            limit=10 * MIB,
        )
        maps.append(sent)
        drives.append(own)
        solved.append(yt)
        maps_other.append(lax.ppermute(sent, "seq", pairs))
    readers = [make_readers(range(6), normed, w_query[0], kt, rt, rb, *solved)]
    maps_other, readers = lax.optimization_barrier((maps_other, readers))

    chip_maps = plain_call(
        compose_kernel,
        "compose",
        shape(VH, 2 * HALF, DK),
        10**9,
        5 * 2**20,
        (core, *maps, *drives, *maps_other),
    )
    gathered = lax.all_to_all(chip_maps, "seq", 0, 0, axis_index_groups=groups)
    gathered_other = lax.ppermute(gathered[:, :HALF], "seq", pairs)
    rt, gathered = lax.optimization_barrier((rt, gathered))
    readers.append(make_readers(range(6, KH), normed, w_query[0], kt, rt, rb, *solved))
    gathered_other, readers = lax.optimization_barrier((gathered_other, readers))
    states = plain_call(
        scan_kernel,
        "scan_chips",
        shape(chips, HALF, DK),
        10**8,
        30 * 2**20,
        (core, gathered, gathered_other, initial),
    )
    returned = lax.all_to_all(states, "seq", 0, 0, axis_index_groups=groups)
    keep, send = plain_call(
        enter_kernel,
        "enter",
        [shape(VH, HALF, DK)] * 2,
        10**9,
        30 * 2**20,
        (core, returned, *maps, *drives, *maps_other),
    )
    got = lax.ppermute(send, "seq", pairs)
    locals_, readers_ = zip(*readers)
    sections = lax.axis_size("section")
    onward = [(i, (i + 1) % sections) for i in range(sections)]
    chunk = T // CHUNKS
    arrived = []
    for part in range(PARTS):
        rows_out = plain_call(
            functools.partial(output_kernel, part),
            "output_rows",
            shape(T // PARTS, x.shape[1]),
            10**9,
            8 * 2**20,
            (core, keep, got, head_gain, x, w_output[0], *locals_, *readers_),
        )
        for i in range(0, T // PARTS, chunk):
            arrived.append(lax.ppermute(rows_out[i : i + chunk], "section", onward))
    next_rows = jnp.concatenate(arrived)
    boundary = plain_call(
        boundary_kernel, "boundary", shape(VH, DK, DV), 10**9, 4 * 2**20, (core, keep, got, *maps, *drives)
    )
    return (next_rows[None], boundary[None, None])


def solution(mesh):
    placed = (
        P("section", "seq", None),
        P("section", None),
        P("section", None, None),
        P("section", None, None),
        P("section", None, None),
        P("section", None, None),
        P("section", None, None),
        P("section", None),
        P("section", None),
        P("section", None),
        P("section", None),
        P("section", None, None),
        P("section", None, None, None),
    )
    return jax.shard_map(
        on_device,
        mesh=mesh,
        in_specs=placed,
        out_specs=(P("section", "seq", None), P("section", "seq", None, None, None)),
        check_vma=False,
    )
```

```python
import functools

import jax
import jax.numpy as jnp
from jax import lax
from jax.experimental import pallas as pl
from jax.experimental.pallas import tpu as pltpu
from jax.sharding import PartitionSpec as P

KH = 8
VH = 16
DK = 128
DV = 128
T = 128
HALF = 64
CHUNKS = 4
PARTS = 1
SPLIT = 2
f32 = jnp.float32
bf16 = jnp.bfloat16
HIGHEST = lax.Precision.HIGHEST
MIB = 2**20
BATCH = 4


def parts(values):
    high = values.astype(bf16)
    return high, (values - high.astype(f32)).astype(bf16)


def left_parts(values):
    return jnp.concatenate(parts(values), axis=1)


def right_parts(values):
    both = jnp.concatenate(parts(values), axis=1)
    return jnp.concatenate([both, both], axis=0)


def mm_parts(left, right):
    both = jnp.dot(left, right, preferred_element_type=f32)
    columns = both.shape[1] // 2
    return both[:, :columns] + both[:, columns:]


def mm(left, right):
    return mm_parts(left_parts(left), right_parts(right))


def mm_t(left, right):
    high, low = parts(left)
    right_high, right_low = parts(right)
    return dot_t(
        jnp.concatenate([high, low, high], axis=1),
        jnp.concatenate([right_high, right_high, right_low], axis=1),
    )


def dot_t(left, right):
    return lax.dot_general(left, right, (((1,), (1,)), ((), ())), preferred_element_type=f32)


def sigmoid(values):
    return 1.0 / (1.0 + jnp.exp(-values))


def silu(values):
    return values * sigmoid(values)


def softplus(values):
    return jnp.maximum(values, 0.0) + jnp.log1p(jnp.exp(-jnp.abs(values)))


def unit(values):
    return values * lax.rsqrt(jnp.sum(values * values, axis=-1, keepdims=True) + 1e-06)


def square_iotas():
    rows = lax.broadcasted_iota(jnp.int32, (T, T), 0)
    columns = lax.broadcasted_iota(jnp.int32, (T, T), 1)
    return rows, columns


def upper_inverses(uppers):
    rows, columns = square_iotas()
    identity = (rows == columns).astype(f32)
    inside = (rows >> 3) == (columns >> 3)
    small = [jnp.where(inside, u, 0.0) for u in uppers]
    squares = [mm(n, n) for n in small]
    stacked = [mm(jnp.concatenate([s, n], axis=0), s) for s, n in zip(squares, small)]
    firsts = [identity - n + s - z[T:] for n, s, z in zip(small, squares, stacked)]
    result = [p + mm(p, z[:T]) for p, z in zip(firsts, stacked)]
    upper_lefts = [left_parts(u) for u in uppers]
    rows, columns = jnp.concatenate([rows, rows], axis=1), jnp.concatenate([columns, columns], axis=1)
    for shift in (3, 4, 5, 6):
        off = ((rows >> (shift + 1)) == (columns >> (shift + 1))) & (
            (rows >> shift) != (columns >> shift)
        )
        off = off.astype(f32).astype(bf16)
        lefts = [left_parts(w) for w in result]
        rights = [right_parts(w) for w in result]
        middles = [mm_parts(off * u, r) for u, r in zip(upper_lefts, rights)]
        result = [
            w - mm_parts(left, right_parts(m)) for w, left, m in zip(result, lefts, middles)
        ]
    return result


def masks_kernel(core_ref, out_ref):
    rows, columns = square_iotas()
    out_ref[0] = (rows <= columns).astype(f32)
    out_ref[1] = (rows == columns).astype(f32)


def column_of(row_ref):
    rows = lax.broadcasted_iota(jnp.int32, (VH, VH), 0)
    columns = lax.broadcasted_iota(jnp.int32, (VH, VH), 1)
    return jnp.sum(jnp.where(rows == columns, row_ref[...], 0.0), axis=1, keepdims=True)


def norm_kernel(
    core_ref,
    mask_ref,
    x_ref,
    gain_ref,
    wb_ref,
    wd_ref,
    rate_ref,
    dtb_ref,
    bb_ref,
    normed_ref,
    bt_ref,
    rt_ref,
    rb_ref,
):
    x = x_ref[...]
    mean_square = jnp.mean(x * x, axis=-1, keepdims=True)
    normed = (x * lax.rsqrt(mean_square + 1e-06) * gain_ref[...]).astype(bf16)
    normed_ref[...] = normed
    bt_ref[...] = sigmoid(dot_t(wb_ref[...], normed) + column_of(bb_ref))
    log_decay = -jnp.exp(column_of(rate_ref)) * softplus(
        dot_t(wd_ref[...], normed) + column_of(dtb_ref)
    )
    running = jnp.dot(log_decay, mask_ref[0], precision=HIGHEST, preferred_element_type=f32)
    rt_ref[...] = running
    for h in range(VH):
        rb_ref[h] = jnp.broadcast_to(running[h : h + 1], (T, T)).T


def inverses_kernel(
    core_ref, normed_ref, bt_ref, rt_ref, rb_ref, wk_ref, keys_ref, kt_ref, inverse_ref
):
    rows, columns = square_iotas()
    key_all = silu(jnp.dot(normed_ref[...], wk_ref[...], preferred_element_type=f32))
    keys = [unit(key_all[:, i * DK : (i + 1) * DK]) for i in range(KH)]
    keys_t = [k.T for k in keys]
    for i in range(KH):
        keys_ref[i] = keys[i]
        kt_ref[i] = keys_t[i]
    grams = [mm(k, kt) for k, kt in zip(keys, keys_t)]
    strict = rows < columns
    uppers = []
    for h in range(VH):
        spread = jnp.minimum(rt_ref[h : h + 1] - rb_ref[h], 0.0)
        uppers.append(jnp.where(strict, bt_ref[h : h + 1] * jnp.exp(spread) * grams[h // 2], 0.0))
    for h, inverse in enumerate(upper_inverses(uppers)):
        inverse_ref[h] = inverse


def maps_kernel(
    part,
    core_ref,
    mask_ref,
    normed_ref,
    bt_ref,
    rt_ref,
    wv_ref,
    keys_ref,
    kt_ref,
    inverse_ref,
    send_ref,
    own_ref,
    yt_ref,
):
    span = VH // SPLIT
    columns = slice(part * span * DV, (part + 1) * span * DV)
    value_all = silu(jnp.dot(normed_ref[...], wv_ref[:, columns], preferred_element_type=f32))
    other_rows = pl.ds(pl.multiple_of((1 - core_ref[0]) * HALF, HALF), HALF)
    for n in range(span):
        h = part * span + n
        i = h // 2
        key_right = right_parts(keys_ref[i])
        r_row, b_row = rt_ref[h : h + 1], bt_ref[h : h + 1]
        value_t = value_all[:, n * DV : (n + 1) * DV].T
        right_t = jnp.concatenate([b_row * value_t, (b_row * jnp.exp(r_row)) * kt_ref[i]], axis=0)
        solved = mm(right_t, inverse_ref[h])
        yt_ref[n] = solved
        end = r_row[:, T - 1 : T]
        both = mm_parts(left_parts(solved * jnp.exp(end - r_row)), key_right)
        own_ref[n] = both[:DV]
        send_ref[n, 0:DK] = jnp.exp(end) * mask_ref[1] - both[DV:]
        send_ref[n, DK : DK + HALF] = own_ref[n, other_rows, :]


def of_head(refs, h):
    span = VH // len(refs)
    return refs[h // span].at[h % span]


def readers_kernel(
    normed_ref, wq_ref, kt_ref, rt_ref, rb_ref, *refs
):
    yt_refs, (local_ref, reader_ref) = refs[:SPLIT], refs[SPLIT:]
    rows, columns = square_iotas()
    inclusive = rows >= columns
    query_all = silu(jnp.dot(normed_ref[...], wq_ref[...], preferred_element_type=f32))
    for i in range(KH):
        query = unit(query_all[:, i * DK : (i + 1) * DK]) * DK ** (-0.5)
        product = mm(query, kt_ref[i])
        for h in (2 * i, 2 * i + 1):
            spread = jnp.minimum(rb_ref[h] - rt_ref[h : h + 1], 0.0)
            both = mm_t(jnp.where(inclusive, jnp.exp(spread) * product, 0.0), of_head(yt_refs, h)[...])
            local_ref[h] = both[:, :DV]
            reader_ref[h] = jnp.exp(rb_ref[h]) * query - both[:, DV:]


def make_readers(normed, wq, *arguments):
    vmem = pl.BlockSpec(memory_space=pltpu.VMEM)
    return pl.pallas_call(
        readers_kernel,
        in_specs=[vmem] * (2 + len(arguments)),
        out_specs=[vmem, vmem],
        out_shape=[jax.ShapeDtypeStruct((VH, T, T), f32)] * 2,
        compiler_params=pltpu.CompilerParams(vmem_limit_bytes=8 * MIB),
        cost_estimate=pl.CostEstimate(
            flops=2 * 10**9, bytes_accessed=8 * 2**20, transcendentals=10**6
        ),
        name="readers",
    )(normed, wq, *arguments)


def on_each_core(core_ref, body):
    for core in (0, 1):

        @pl.when(core_ref[0] == core)
        def _(core=core):
            body(core)


def initial_kernel(place_ref, carry_ref, out_ref):
    state = carry_ref[place_ref[0]].T

    @pl.when(place_ref[1] == 0)
    def _():
        out_ref[...] = state[:HALF]

    @pl.when(place_ref[1] == 1)
    def _():
        out_ref[...] = state[HALF:]


def compose_kernel(core_ref, *refs):
    sent_refs, own_refs, got_refs = (refs[n * SPLIT : (n + 1) * SPLIT] for n in range(3))
    out_ref = refs[-1]

    def body(core):
        mine = slice(core * HALF, core * HALF + HALF)
        for h in range(VH):
            sent, own, got = (of_head(r, h) for r in (sent_refs, own_refs, got_refs))
            own_b, got_b = own[mine], got[DK : DK + HALF]
            if core == 0:
                first_a, first_b, second_a, second_b = sent, own_b, got, got_b
            else:
                first_a, first_b, second_a, second_b = got, got_b, sent, own_b
            both = mm(jnp.concatenate([first_a[mine], first_b], axis=0), second_a[0:DK])
            out_ref[h, 0:HALF] = both[:HALF]
            out_ref[h, HALF : 2 * HALF] = both[HALF:] + second_b

    on_each_core(core_ref, body)


def scan_kernel(core_ref, map_ref, other_ref, initial_ref, out_ref):

    def body(core):
        count = map_ref.shape[0]

        def full(p):
            halves = [map_ref[p, 0:HALF], other_ref[p]]
            return jnp.concatenate(halves if core == 0 else halves[::-1], axis=0)

        drive = lambda p: map_ref[p, HALF : 2 * HALF]
        def after(first, second):
            both = mm(jnp.concatenate(first, axis=0), second[0])
            return both[:DK], both[DK:] + second[1]

        apply = lambda state, move: mm(state, move[0]) + move[1]
        single = [(full(p), drive(p)) for p in range(count)]
        pairs = [after(single[p], single[p + 1]) for p in range(0, count - 2, 2)]
        fours = [after(pairs[n], pairs[n + 1]) for n in range(0, len(pairs) - 1, 2)]
        current = initial_ref[...]
        for p in range(0, count, 4):
            middle = apply(current, pairs[p // 2])
            out_ref[p] = current
            out_ref[p + 1] = apply(current, single[p])
            out_ref[p + 2] = middle
            out_ref[p + 3] = apply(middle, single[p + 2])
            if p < count - 4:
                current = apply(current, fours[p // 4])

    on_each_core(core_ref, body)


def enter_kernel(core_ref, state_ref, *refs):
    sent_refs, own_refs, got_refs = (refs[n * SPLIT : (n + 1) * SPLIT] for n in range(3))
    keep_ref, send_ref = refs[3 * SPLIT :]

    def body(core):
        given, moved = (keep_ref, send_ref) if core == 0 else (send_ref, keep_ref)
        for h in range(VH):
            sent, own, got = (of_head(r, h) for r in (sent_refs, own_refs, got_refs))
            state = state_ref[h]
            given[h] = state
            if core == 0:
                moved[h] = mm(state, sent[0:DK]) + own[0:HALF]
            else:
                moved[h] = mm(state, got[0:DK]) + got[DK : DK + HALF]

    on_each_core(core_ref, body)


def entering_of(core_ref, keep_ref, got_ref, h):
    keep, got = keep_ref[h], got_ref[h]
    first = core_ref[0] == 0
    return jnp.concatenate([jnp.where(first, keep, got), jnp.where(first, got, keep)], axis=0)


def output_kernel(
    part, core_ref, keep_ref, got_ref, local_ref, reader_ref, gain_ref, x_ref, wo_ref, out_ref
):
    rows = slice(part * T // PARTS, (part + 1) * T // PARTS)
    heads = []
    for h in range(VH):
        entering = entering_of(core_ref, keep_ref, got_ref, h)
        core = local_ref[h, rows] + mm_t(reader_ref[h, rows], entering)
        mean_square = jnp.mean(core * core, axis=-1, keepdims=True)
        heads.append((core * lax.rsqrt(mean_square + 1e-06) * gain_ref[...]).astype(bf16))
    out_ref[...] = x_ref[rows] + jnp.dot(
        jnp.concatenate(heads, axis=1), wo_ref[...], preferred_element_type=f32
    )


def boundary_kernel(core_ref, keep_ref, got_ref, *refs):
    sent_refs, own_refs, out_ref = refs[:SPLIT], refs[SPLIT : 2 * SPLIT], refs[-1]
    for h in range(VH):
        entering = entering_of(core_ref, keep_ref, got_ref, h)
        sent, own = of_head(sent_refs, h), of_head(own_refs, h)
        out_ref[h] = (mm(entering, sent[0:DK]) + own[...]).T


def plain_call(kernel, name, outputs, flops, bytes_accessed, arguments, limit=6 * MIB):
    vmem = pl.BlockSpec(memory_space=pltpu.VMEM)
    specs = [pl.BlockSpec(memory_space=pltpu.SMEM)] + [vmem] * (len(arguments) - 1)
    several = isinstance(outputs, list)
    return pl.pallas_call(
        kernel,
        in_specs=specs,
        out_specs=[vmem] * len(outputs) if several else vmem,
        out_shape=outputs,
        compiler_params=pltpu.CompilerParams(vmem_limit_bytes=limit),
        cost_estimate=pl.CostEstimate(
            flops=flops, bytes_accessed=bytes_accessed, transcendentals=0
        ),
        name=name,
    )(*arguments)


def on_device(
    stream,
    norm_gain,
    w_query,
    w_key,
    w_value,
    w_beta,
    w_decay,
    a_log,
    dt_bias,
    beta_bias,
    head_gain,
    w_output,
    carry_state,
):
    count = lax.axis_size("seq")
    position = lax.axis_index("seq")
    core = (position % 2).astype(jnp.int32)[None]
    chips = count // 2
    pairs = [(i, i ^ 1) for i in range(count)]
    groups = [[2 * i + c for i in range(chips)] for c in range(2)]
    x = stream[0]
    shape = lambda *dims: jax.ShapeDtypeStruct(dims, f32)

    masks = plain_call(masks_kernel, "masks", shape(2, T, T), 10**11, 200 * 2**20, (core,))
    normed, bt, rt, rb = plain_call(
        norm_kernel,
        "norm_and_gates",
        [jax.ShapeDtypeStruct(x.shape, bf16), shape(VH, T), shape(VH, T), shape(VH, T, T)],
        10**9,
        100 * 2**20,
        (
            core,
            masks,
            x,
            norm_gain,
            w_beta[0].T,
            w_decay[0].T,
            a_log,
            dt_bias,
            beta_bias,
        ),
    )
    place = jnp.stack([position // 2, position % 2]).astype(jnp.int32)
    place, normed = lax.optimization_barrier((place, normed))
    initial = plain_call(
        initial_kernel, "initial_state", shape(HALF, DK), 10**6, 2**20, (place, carry_state[0])
    )
    keys, kt, inverses = plain_call(
        inverses_kernel,
        "inverses",
        [shape(KH, T, DK), shape(KH, DK, T), shape(VH, T, T)],
        2 * 10**9,
        20 * 2**20,
        (core, normed, bt, rt, rb, w_key[0]),
        limit=20 * MIB,
    )
    span = VH // SPLIT
    maps, drives, solved, maps_other = [], [], [], []
    for part in range(SPLIT):
        sent, own, yt = plain_call(
            functools.partial(maps_kernel, part),
            "block_maps",
            [shape(span, DK + HALF, DK), shape(span, DV, DK), shape(span, DK + DV, T)],
            2 * 10**9,
            10 * 2**20,
            (core, masks, normed, bt, rt, w_value[0], keys, kt, inverses),
            limit=10 * MIB,
        )
        maps.append(sent)
        drives.append(own)
        solved.append(yt)
        maps_other.append(lax.ppermute(sent, "seq", pairs))
    local, reader = make_readers(normed, w_query[0], kt, rt, rb, *solved)
    maps_other, local, reader = lax.optimization_barrier((maps_other, local, reader))

    chip_maps = plain_call(
        compose_kernel,
        "compose",
        shape(VH, 2 * HALF, DK),
        10**9,
        5 * 2**20,
        (core, *maps, *drives, *maps_other),
    )
    gathered = lax.all_to_all(chip_maps, "seq", 0, 0, axis_index_groups=groups)
    gathered_other = lax.ppermute(gathered[:, :HALF], "seq", pairs)
    states = plain_call(
        scan_kernel,
        "scan_chips",
        shape(chips, HALF, DK),
        10**8,
        30 * 2**20,
        (core, gathered, gathered_other, initial),
    )
    returned = lax.all_to_all(states, "seq", 0, 0, axis_index_groups=groups)
    keep, send = plain_call(
        enter_kernel,
        "enter",
        [shape(VH, HALF, DK)] * 2,
        10**9,
        30 * 2**20,
        (core, returned, *maps, *drives, *maps_other),
    )
    got = lax.ppermute(send, "seq", pairs)
    sections = lax.axis_size("section")
    onward = [(i, (i + 1) % sections) for i in range(sections)]
    chunk = T // CHUNKS
    arrived = []
    for part in range(PARTS):
        rows_out = plain_call(
            functools.partial(output_kernel, part),
            "output_rows",
            shape(T // PARTS, x.shape[1]),
            10**9,
            8 * 2**20,
            (core, keep, got, local, reader, head_gain, x, w_output[0]),
        )
        for i in range(0, T // PARTS, chunk):
            arrived.append(lax.ppermute(rows_out[i : i + chunk], "section", onward))
    next_rows = jnp.concatenate(arrived)
    boundary = plain_call(
        boundary_kernel, "boundary", shape(VH, DK, DV), 10**9, 4 * 2**20, (core, keep, got, *maps, *drives)
    )
    return (next_rows[None], boundary[None, None])


def solution(mesh):
    placed = (
        P("section", "seq", None),
        P("section", None),
        P("section", None, None),
        P("section", None, None),
        P("section", None, None),
        P("section", None, None),
        P("section", None, None),
        P("section", None),
        P("section", None),
        P("section", None),
        P("section", None),
        P("section", None, None),
        P("section", None, None, None),
    )
    return jax.shard_map(
        on_device,
        mesh=mesh,
        in_specs=placed,
        out_specs=(P("section", "seq", None), P("section", "seq", None, None, None)),
        check_vma=False,
    )
```
